32 devices in a mesh: sec: 2 (over y), dev: 16 (over z, x, core).
Axes of the slice: x: 2, y: 2, z: 4, core: 2. Of those that a mesh axis runs over, the one named last changes fastest.
Arguments:
- sources: float32 [2, 8, 8192], P(None, None, ('sec', 'dev')), may hold values from -16 to 16
- positions: float32 [3, 8192], P(None, ('sec', 'dev')), may hold values from -0.5 to 16, as said below
- weights: float32 [8192], P(('sec', 'dev')), may hold values from 0.5 to 2
- wavenumbers: float32 [8], replicated, may hold values from 1 to 8
- directions: float32 [3, 128], replicated, may hold values from -1 to 1
- box_centers: float32 [3, 32], replicated, may hold values from -0.25 to 16
- group_centers: float32 [3, 4], replicated, may hold values from -0.25 to 16
- near_pairs: int32 [32, 2, 10], P(('sec', 'dev')), may hold values from 0 to 5, as said below
- pair_counts: int32 [32], P(('sec', 'dev')), may hold values from 3 to 10, as said below
- box_lists: int32 [32, 4], P(('sec', 'dev')), may hold values from 0 to 31, as said below
- group_lists: int32 [4, 2], replicated, may hold values from 0 to 3, as said below
Outputs:
- result: float32 [2, 8, 8192], P(None, None, ('sec', 'dev'))
- rayleigh: float32 [2, 8], replicated
The draws below stay inside these ranges and needn't reach their ends.
Inputs may be any that keep to these rules, and one draw needn't show every extreme that they name: `positions`: panels of leaf l lie within half a unit of a grid point of a 16 by 16 layered grid, leaves in order along it. `near_pairs`: row 0 holds leaves of the device's own box, row 1 leaves of its window; the first three pairs of every device take a source leaf of the box before, of the box after, and the target leaf itself. `pair_counts`: some device has all 10 pairs live. `box_lists`: A row holds distinct boxes, never the box itself or the ones just before and after it. `group_lists`: A row holds distinct groups other than the group itself.
All inputs are finite; a program needn't handle non-finite values.
Results may differ from the reference program's by a relative error of at most 0.0003.
Values sent between devices are 32-bit elements; how exact they have to be, the bound alone decides.
A program may use at most 64 MiB of HBM per device.

```python
import math
import jax
import jax.numpy as jnp
from jax import lax

LEAF = 128
LEAVES = 2
F = 8
Q = 128
PAIRS_LEAF = 5
ML1 = 4
ML2 = 2
GROUP = 8
P_DEV = 256
PAIRS_MAX = 10
PANELS = 8192
GROUPS = 4
DEVICES = 32


def leaf_grid(leaf_ids):
    grid_column = (leaf_ids % 16).astype(jnp.float32)
    grid_row = (leaf_ids // 16 % 16).astype(jnp.float32)
    grid_layer = (leaf_ids // 256).astype(jnp.float32)
    return jnp.stack([grid_column, grid_row, grid_layer])


def draw_sources(key, part):
    panel_ramp = jnp.arange(PANELS, dtype=jnp.float32) / PANELS
    samples = jnp.clip(jax.random.normal(key, (2, F, PANELS), jnp.float32), -4.0, 4.0)
    return samples * (1.0 + 2.0 * panel_ramp)


def draw_positions(key, part):
    leaf_ids = jnp.arange(PANELS, dtype=jnp.int32) // LEAF
    jitter = jax.random.uniform(key, (3, PANELS), jnp.float32, -0.5, 0.5)
    return leaf_grid(leaf_ids) + jitter


def draw_box_centers(key, part):
    leaf_ids = jnp.arange(DEVICES, dtype=jnp.int32)[:, None] * LEAVES + jnp.arange(LEAVES, dtype=jnp.int32)[None, :]
    mean_xyz = jnp.mean(leaf_grid(leaf_ids), axis=2)
    return mean_xyz + jax.random.uniform(key, (3, DEVICES), jnp.float32, -0.25, 0.25)


def draw_group_centers(key, part):
    leaf_ids = jnp.arange(GROUPS, dtype=jnp.int32)[:, None] * (GROUP * LEAVES) + jnp.arange(GROUP * LEAVES, dtype=jnp.int32)[None, :]
    mean_xyz = jnp.mean(leaf_grid(leaf_ids), axis=2)
    return mean_xyz + jax.random.uniform(key, (3, GROUPS), jnp.float32, -0.25, 0.25)


def draw_near_pairs(key, part):
    subkeys = jax.random.split(jax.random.fold_in(key, 11), 4)
    targets = jax.random.randint(subkeys[0], (DEVICES, PAIRS_MAX), 0, LEAVES)
    anchors = jax.random.randint(subkeys[1], (DEVICES, PAIRS_MAX), 0, 3 * LEAVES)
    preceding = jax.random.randint(subkeys[2], (DEVICES,), 0, LEAVES)
    following = jax.random.randint(subkeys[3], (DEVICES,), 2 * LEAVES, 3 * LEAVES)
    anchors = anchors.at[:, 0].set(preceding).at[:, 1].set(following).at[:, 2].set(targets[:, 2] + LEAVES)
    return jnp.stack([targets, anchors], axis=1).astype(jnp.int32)


def draw_pair_counts(key, part):
    subkeys = jax.random.split(jax.random.fold_in(key, 23), 3)
    lowest = max(3, PAIRS_MAX // 4)
    counts = jax.random.randint(subkeys[0], (DEVICES,), lowest, PAIRS_MAX + 1)
    fullest = jax.random.randint(subkeys[1], (), 0, DEVICES)
    emptiest = (fullest + 1 + jax.random.randint(subkeys[2], (), 0, DEVICES - 1)) % DEVICES
    return counts.at[fullest].set(PAIRS_MAX).at[emptiest].set(lowest).astype(jnp.int32)


def draw_box_lists(key, part):
    subkeys = jax.random.split(jax.random.fold_in(key, 37), DEVICES)
    offsets = jax.vmap(lambda row_key: jax.random.permutation(row_key, DEVICES - 3)[:ML1])(subkeys) + 2
    return ((jnp.arange(DEVICES, dtype=jnp.int32)[:, None] + offsets) % DEVICES).astype(jnp.int32)


def draw_group_lists(key, part):
    subkeys = jax.random.split(jax.random.fold_in(key, 41), GROUPS)
    offsets = jax.vmap(lambda row_key: jax.random.permutation(row_key, GROUPS - 1)[:ML2])(subkeys) + 1
    return ((jnp.arange(GROUPS, dtype=jnp.int32)[:, None] + offsets) % GROUPS).astype(jnp.int32)


def block_levels(key, dims, cuts, least, high):
    level, own = 1.0, jax.random.fold_in(key, 6)
    for dim, blocks in cuts:
        draws = jnp.exp(jax.random.uniform(jax.random.fold_in(own, dim), (blocks,), jnp.float32, least / len(cuts), high / len(cuts)))
        level = level * jnp.repeat(draws, dims[dim] // blocks).reshape([-1 if axis == dim else 1 for axis in range(len(dims))])
    return level


def setup_inputs(seed: int = 0) -> dict:
    arg_keys = jax.random.split(jax.random.key(seed), 12)
    return {
        "sources": draw_sources(jax.random.fold_in(arg_keys[11], 71), 0),
        "positions": draw_positions(jax.random.fold_in(arg_keys[11], 71), 0),
        "weights": jnp.clip(jnp.exp(math.log(2.0) - 1.3862944 * jax.random.uniform(arg_keys[2], (PANELS,), jnp.float32) ** block_levels(arg_keys[2], (PANELS,), ((0, 32),), -0.2, 0.2)), 0.5, 2.0),
        "wavenumbers": jnp.clip(jnp.exp(jax.random.uniform(arg_keys[3], (F,), jnp.float32, math.log(1.0), math.log(8.0))), 1.0, 8.0),
        "directions": jnp.clip(jax.random.uniform(arg_keys[4], (3, Q), jnp.float32, -1.0, 1.0), -1.0, 1.0),
        "box_centers": draw_box_centers(jax.random.fold_in(arg_keys[11], 71), 0),
        "group_centers": draw_group_centers(jax.random.fold_in(arg_keys[11], 71), 0),
        "near_pairs": draw_near_pairs(jax.random.fold_in(arg_keys[11], 71), 0),
        "pair_counts": draw_pair_counts(jax.random.fold_in(arg_keys[11], 71), 0),
        "box_lists": draw_box_lists(jax.random.fold_in(arg_keys[11], 71), 0),
        "group_lists": draw_group_lists(jax.random.fold_in(arg_keys[11], 71), 0),
    }


SOFT = 0.1

def kernel_block(targets_xyz, sources_xyz, wave_numbers, reach_scale):
    offsets = targets_xyz[:, :, None] - sources_xyz[:, None, :]
    distance = jnp.sqrt(lax.optimization_barrier(jnp.sum(offsets * offsets, axis=0)) + SOFT * SOFT)
    amplitude = reach_scale / distance
    phases = wave_numbers[:, None, None] * distance[None, :, :]
    return (amplitude[None] * jnp.cos(phases), amplitude[None] * jnp.sin(phases))

def apply_block(kernel, values):
    real_kernel, imag_kernel = kernel
    highest = lax.Precision.HIGHEST
    real_real = jnp.einsum('fab,fb->fa', real_kernel, values[0], precision=highest)
    imag_imag = jnp.einsum('fab,fb->fa', imag_kernel, values[1], precision=highest)
    real_imag = jnp.einsum('fab,fb->fa', real_kernel, values[1], precision=highest)
    imag_real = jnp.einsum('fab,fb->fa', imag_kernel, values[0], precision=highest)
    return jnp.stack([real_real - imag_imag, real_imag + imag_real])

def upward(group_index, box_centers, group_centers, directions, wave_numbers, multipoles, radius_box, radius_group):
    children = group_index * GROUP + jnp.arange(GROUP, dtype=jnp.int32)
    parent_proxies = lax.dynamic_index_in_dim(group_centers, group_index, 1, keepdims=False)[:, None] + radius_group * directions
    child_proxies = box_centers[:, children][:, :, None] + radius_box * directions[:, None, :]
    kernels = jax.vmap(kernel_block, in_axes=(None, 1, None, None))(parent_proxies, child_proxies, wave_numbers, radius_group)
    return jax.vmap(apply_block)(kernels, multipoles[children]).sum(0) / math.sqrt(GROUP * Q)

def reference(sources, positions, weights, wavenumbers, directions, box_centers, group_centers, near_pairs, pair_counts, box_lists, group_lists):
    radius_box = 1.0 + 0.5 * LEAVES
    radius_group = 2.0 * radius_box
    weighted = sources * weights[None, None, :]

    def box_proxies(index):
        return lax.dynamic_index_in_dim(box_centers, index, 1, keepdims=False)[:, None] + radius_box * directions

    def outgoing(device):
        first_panel = (device * P_DEV).astype(jnp.int32)
        local_xyz = lax.dynamic_slice_in_dim(positions, first_panel, P_DEV, 1)
        local_values = lax.dynamic_slice_in_dim(weighted, first_panel, P_DEV, 2)
        kernel = kernel_block(box_proxies(device), local_xyz, wavenumbers, radius_box)
        return apply_block(kernel, local_values) / math.sqrt(P_DEV)
    box_multipoles = lax.map(outgoing, jnp.arange(DEVICES, dtype=jnp.int32))

    def group_outgoing(group_index):
        return upward(group_index, box_centers, group_centers, directions, wavenumbers, box_multipoles, radius_box, radius_group)
    group_multipoles = lax.map(group_outgoing, jnp.arange(GROUPS, dtype=jnp.int32))
    padded_values = jnp.pad(weighted, ((0, 0), (0, 0), (P_DEV, P_DEV)))
    padded_xyz = jnp.pad(positions, ((0, 0), (P_DEV, P_DEV)))

    def respond(device):
        first_panel = (device * P_DEV).astype(jnp.int32)
        window_xyz = lax.dynamic_slice_in_dim(padded_xyz, first_panel, 3 * P_DEV, 1)
        window_values = lax.dynamic_slice_in_dim(padded_values, first_panel, 3 * P_DEV, 2)
        local_xyz = lax.dynamic_slice_in_dim(positions, first_panel, P_DEV, 1)
        local_sources = lax.dynamic_slice_in_dim(sources, first_panel, P_DEV, 2)
        device_pairs = near_pairs[device]
        live_count = pair_counts[device]

        def near_step(near_total, pair_index):
            target_leaf = (device_pairs[0, pair_index] * LEAF).astype(jnp.int32)
            anchor_leaf = (device_pairs[1, pair_index] * LEAF).astype(jnp.int32)
            target_xyz = lax.dynamic_slice_in_dim(local_xyz, target_leaf, LEAF, 1)
            anchor_xyz = lax.dynamic_slice_in_dim(window_xyz, anchor_leaf, LEAF, 1)
            anchor_values = lax.dynamic_slice_in_dim(window_values, anchor_leaf, LEAF, 2)
            near_block = apply_block(kernel_block(target_xyz, anchor_xyz, wavenumbers, 1.0), anchor_values)
            near_block = jnp.where(pair_index < live_count, near_block, jnp.zeros_like(near_block))
            existing = lax.dynamic_slice_in_dim(near_total, target_leaf, LEAF, 2)
            return (lax.dynamic_update_slice_in_dim(near_total, existing + near_block, target_leaf, 2), None)
        near_total, _ = lax.scan(near_step, jnp.zeros((2, F, P_DEV), jnp.float32), jnp.arange(PAIRS_MAX, dtype=jnp.int32))
        own_proxies = box_proxies(device)
        source_boxes = box_lists[device]
        source_proxies = box_centers[:, source_boxes][:, :, None] + radius_box * directions[:, None, :]
        kernels = jax.vmap(kernel_block, in_axes=(None, 1, None, None))(own_proxies, source_proxies, wavenumbers, radius_box)
        incoming = jax.vmap(apply_block)(kernels, box_multipoles[source_boxes]).sum(0) / math.sqrt(ML1 * Q)
        parent = (device // GROUP).astype(jnp.int32)
        parent_proxies = lax.dynamic_index_in_dim(group_centers, parent, 1, keepdims=False)[:, None] + radius_group * directions
        source_groups = group_lists[parent]
        group_proxies = group_centers[:, source_groups][:, :, None] + radius_group * directions[:, None, :]
        group_kernels = jax.vmap(kernel_block, in_axes=(None, 1, None, None))(parent_proxies, group_proxies, wavenumbers, radius_group)
        group_local = jax.vmap(apply_block)(group_kernels, group_multipoles[source_groups]).sum(0) / math.sqrt(ML2 * Q)
        descended = apply_block(kernel_block(own_proxies, parent_proxies, wavenumbers, radius_group), group_local) / math.sqrt(Q)
        box_local = incoming + descended
        far_field = apply_block(kernel_block(local_xyz, own_proxies, wavenumbers, radius_box), box_local) / math.sqrt(Q)
        return 0.5 * local_sources + near_total / math.sqrt(LEAF * PAIRS_LEAF) + far_field
    pieces = lax.map(respond, jnp.arange(DEVICES, dtype=jnp.int32))
    result = jnp.transpose(pieces, (1, 2, 0, 3)).reshape(2, F, PANELS)
    denominator = lax.optimization_barrier(jnp.sum(sources[0] * sources[0] + sources[1] * sources[1], axis=-1)) + 1e-06
    real_sum = lax.optimization_barrier(jnp.sum(sources[0] * result[0] + sources[1] * result[1], axis=-1))
    imag_sum = lax.optimization_barrier(jnp.sum(sources[0] * result[1] - sources[1] * result[0], axis=-1))
    rayleigh = jnp.stack([real_sum / denominator, imag_sum / denominator])
    return (result, rayleigh)
```

```python
import functools
import math

import jax
import jax.numpy as jnp
from jax import lax
from jax.experimental import pallas as pl
from jax.experimental.pallas import tpu as pltpu
from jax.sharding import PartitionSpec as P

LEAF = 128
LEAVES = 2
F = 8
Q = 128
PAIRS_LEAF = 5
ML1 = 4
ML2 = 2
GROUP = 8
P_DEV = 256
PAIRS_MAX = 10

SOFT = 0.1
RADIUS_BOX = 1.0 + 0.5 * LEAVES
RADIUS_GROUP = 2.0 * RADIUS_BOX
ROWS = 2 * F
REC = 24
BLOCK = 32
ROUNDER = 12582912.0

COS = (
    0.9999992216144897,
    -19.738982519159087,
    64.9287266658944,
    -85.27239730229532,
    58.794039342441934,
    -21.076782244925596,
)
SIN = (
    6.283055797987737,
    -41.33121426662637,
    81.36681462152343,
    -74.47800045497374,
    32.7813926131928,
)
MESH = pl.DeviceIdType.MESH


def horner(coefficients, z):
    total = coefficients[-1]
    for coefficient in coefficients[-2::-1]:
        total = total * z + coefficient
    return total


def geometry(target, cols):
    squared = SOFT * SOFT
    for axis in range(3):
        offset = target[axis] - cols[:, ROWS + axis : ROWS + axis + 1]
        squared = squared + offset * offset
    inverse = lax.rsqrt(squared)
    distance = squared * inverse
    distance = distance + (0.5 * inverse) * (squared - distance * distance)
    return distance, inverse


def point_terms(distance, inverse, turns, real, imag):
    phase = distance * turns
    phase = phase - ((phase + ROUNDER) - ROUNDER)
    z = phase * phase
    cosine = inverse * horner(COS, z)
    sine = (inverse * phase) * horner(SIN, z)
    return cosine * real - sine * imag, cosine * imag + sine * real


def fold(block):
    return block.reshape(block.shape[0] // 8, 8, block.shape[1]).sum(0)


def zeros_acc(count):
    return tuple(jnp.zeros((8, 128), jnp.float32) for _ in range(2 * count))


def apply_points(target, load, turns, acc):
    def step(block, acc):
        cols = load(block)
        distance, inverse = geometry(target, cols)
        out = list(acc)
        for f in range(F):
            re, im = point_terms(
                distance, inverse, turns[f], cols[:, f : f + 1], cols[:, F + f : F + f + 1]
            )
            out[f] = out[f] + fold(re)
            out[F + f] = out[F + f] + fold(im)
        return tuple(out)

    return lax.fori_loop(0, LEAF // BLOCK, step, acc, unroll=True)


def rows_of(acc):
    return jnp.concatenate([jnp.sum(a, axis=0, keepdims=True) for a in acc], axis=0)


def kernel(
    sec_size,
    dev_size,
    groups,
    wave_ref,
    centers_ref,
    group_centers_ref,
    pairs_ref,
    counts_ref,
    lists_ref,
    group_lists_ref,
    sources_ref,
    positions_ref,
    weights_ref,
    directions_ref,
    result_ref,
    rayleigh_ref,
    window,
    records,
    targets_xyz,
    dir_cols,
    scratch_rec,
    multipole,
    gathered,
    contribution,
    contributions,
    group_send,
    group_multipoles,
    local_send,
    group_locals,
    near,
    box_local,
    sums_send,
    sums,
    halo_send_sem,
    halo_recv_sem,
    gather_send_sem,
    gather_recv_sem,
    up_send_sem,
    up_recv_sem,
    across_send_sem,
    across_recv_sem,
    down_send_sem,
    down_recv_sem,
    sums_send_sem,
    sums_recv_sem,
):
    count = sec_size * dev_size
    me = lax.axis_index("sec") * dev_size + lax.axis_index("dev")
    group = me // GROUP
    member = me % GROUP

    def place(device):
        return (device // dev_size, device % dev_size)

    barrier = pltpu.get_barrier_semaphore()

    def greet(step, carry):
        pl.semaphore_signal(
            barrier, inc=1, device_id=place((me + step) % count), device_id_type=MESH
        )
        return carry

    lax.fori_loop(1, count, greet, 0)

    turns = [wave_ref[f] * (0.5 / math.pi) for f in range(F)]

    weighted = sources_ref[...] * weights_ref[...]
    own_rows = jnp.concatenate(
        [weighted, positions_ref[...], jnp.zeros((REC - ROWS - 3, P_DEV), jnp.float32)], axis=0
    )
    window[1] = own_rows
    for leaf in range(LEAVES):
        part = own_rows[:, leaf * LEAF : (leaf + 1) * LEAF]
        records[LEAVES + leaf] = part.T
        targets_xyz[leaf] = part[ROWS : ROWS + 8]
    directions = directions_ref[...]
    dir_rows = jnp.concatenate([directions, jnp.zeros((5, Q), jnp.float32)], axis=0)
    dir_cols[...] = dir_rows.T

    def proxies(centers, index, radius):
        return [centers[axis, index] + radius * directions[axis : axis + 1] for axis in range(3)]

    own_proxies = proxies(centers_ref, me, RADIUS_BOX)
    parent_proxies = proxies(group_centers_ref, group, RADIUS_GROUP)
    row_padding = jnp.zeros((REC - ROWS - 3, Q), jnp.float32)

    def set_records(slot, rows, xyz):
        scratch_rec[slot] = jnp.concatenate([rows, *xyz, row_padding], axis=0).T

    def loader(ref, index):
        return lambda block: ref[index, pl.ds(pl.multiple_of(block * BLOCK, BLOCK), BLOCK), :]

    def outward_leaf(leaf, acc):
        return apply_points(own_proxies, loader(records, LEAVES + leaf), turns, acc)

    outward = lax.fori_loop(0, LEAVES, outward_leaf, zeros_acc(F))
    own_multipole = rows_of(outward) * (RADIUS_BOX / math.sqrt(P_DEV))
    multipole[...] = own_multipole
    gathered[me] = own_multipole

    pl.semaphore_wait(barrier, count - 1)

    after = (me + 1) % count
    before = (me + count - 1) % count
    halos = [
        pltpu.make_async_remote_copy(
            src_ref=window.at[1],
            dst_ref=window.at[slot],
            send_sem=halo_send_sem.at[way],
            recv_sem=halo_recv_sem.at[way],
            device_id=place(device),
            device_id_type=MESH,
        )
        for way, (slot, device) in enumerate(((0, after), (2, before)))
    ]
    for halo in halos:
        halo.start()

    def send_to(src, dst, send_sem, recv_sem, device):
        pltpu.make_async_remote_copy(
            src_ref=src,
            dst_ref=dst,
            send_sem=send_sem,
            recv_sem=recv_sem,
            device_id=place(device),
            device_id_type=MESH,
        ).start()

    def wait_bytes(ref, pieces, sem):
        part = ref.at[pl.ds(0, pieces)]
        pltpu.make_async_copy(part, part, sem).wait()

    def send_multipole(step, carry):
        send_to(
            multipole, gathered.at[me], gather_send_sem, gather_recv_sem, (me + step) % count
        )
        return carry

    set_records(0, own_multipole, own_proxies)
    terms = rows_of(
        apply_points(parent_proxies, loader(scratch_rec, 0), turns, zeros_acc(F))
    ) * (RADIUS_GROUP / math.sqrt(GROUP * Q))
    padding = jnp.zeros((6, Q), jnp.float32)
    for f in range(F):
        contribution[f] = jnp.concatenate(
            [terms[f : f + 1], terms[F + f : F + f + 1], padding], axis=0
        )
    contributions[member] = contribution[member]

    def send_up(step, carry):
        other = (member + step) % GROUP
        send_to(
            contribution.at[other],
            contributions.at[member],
            up_send_sem,
            up_recv_sem,
            group * GROUP + other,
        )
        return carry

    lax.fori_loop(1, GROUP, send_up, 0)
    lax.fori_loop(1, count, send_multipole, 0)

    for way, halo in enumerate(halos):
        halo.wait_recv()
        slot = 2 * way
        inside = jnp.where(me > 0, 1.0, 0.0) if way == 0 else jnp.where(me < count - 1, 1.0, 0.0)
        rows = window[slot]
        rows = jnp.concatenate([rows[:ROWS] * inside, rows[ROWS:]], axis=0)
        for leaf in range(LEAVES):
            records[slot * LEAVES + leaf] = rows[:, leaf * LEAF : (leaf + 1) * LEAF].T
    near[...] = jnp.zeros_like(near)

    def near_pair(pair, carry):
        target = pairs_ref[0, pair]
        anchor = pairs_ref[1, pair]
        live = jnp.where(pair < counts_ref[0], 1.0, 0.0)
        xyz = targets_xyz[target]
        rows = rows_of(
            apply_points(
                [xyz[axis : axis + 1] for axis in range(3)],
                loader(records, anchor),
                turns,
                zeros_acc(F),
            )
        )
        for leaf in range(LEAVES):
            near[leaf] += rows * jnp.where(target == leaf, live, 0.0)
        return carry

    first_half = PAIRS_MAX // 2
    lax.fori_loop(0, first_half, near_pair, 0)

    wait_bytes(contributions, GROUP - 1, up_recv_sem)
    total = contributions[0]
    for other in range(1, GROUP):
        total = total + contributions[other]
    group_send[...] = total
    group_multipoles[group] = total

    def send_across(step, carry):
        send_to(
            group_send,
            group_multipoles.at[group],
            across_send_sem,
            across_recv_sem,
            (me + step * GROUP) % count,
        )
        return carry

    if groups > 1:
        lax.fori_loop(1, groups, send_across, 0)

    lax.fori_loop(first_half, PAIRS_MAX, near_pair, 0)

    if groups > 1:
        wait_bytes(group_multipoles, groups - 1, across_recv_sem)
    my_turns = wave_ref[member] * (0.5 / math.pi)
    local_acc = zeros_acc(1)
    for m in range(ML2):
        other = group_lists_ref[group, m]
        rows = group_multipoles[other]
        xyz = proxies(group_centers_ref, other, RADIUS_GROUP)
        cols = jnp.concatenate([rows, rows, *xyz, row_padding], axis=0).T
        for block in range(Q // BLOCK):
            part = cols[block * BLOCK : (block + 1) * BLOCK]
            distance, inverse = geometry(parent_proxies, part)
            re, im = point_terms(distance, inverse, my_turns, part[:, 0:1], part[:, 1:2])
            local_acc = (local_acc[0] + fold(re), local_acc[1] + fold(im))
    local = jnp.concatenate([rows_of(local_acc), padding], axis=0) * (
        RADIUS_GROUP / math.sqrt(ML2 * Q)
    )
    local_send[...] = local
    group_locals[member] = local

    def send_down(step, carry):
        send_to(
            local_send,
            group_locals.at[member],
            down_send_sem,
            down_recv_sem,
            group * GROUP + (member + step) % GROUP,
        )
        return carry

    lax.fori_loop(1, GROUP, send_down, 0)

    wait_bytes(gathered, count - 1, gather_recv_sem)

    def list_box(m, acc):
        other = lists_ref[0, m]
        set_records(0, gathered[other], proxies(centers_ref, other, RADIUS_BOX))
        return apply_points(own_proxies, loader(scratch_rec, 0), turns, acc)

    incoming = lax.fori_loop(0, ML1, list_box, zeros_acc(F))
    incoming = rows_of(incoming) * (RADIUS_BOX / math.sqrt(ML1 * Q))

    wait_bytes(group_locals, GROUP - 1, down_recv_sem)
    rows = jnp.concatenate(
        [group_locals[f][part : part + 1] for part in range(2) for f in range(F)], axis=0
    )
    set_records(0, rows, parent_proxies)
    descended = rows_of(
        apply_points(own_proxies, loader(scratch_rec, 0), turns, zeros_acc(F))
    ) * (RADIUS_GROUP / math.sqrt(Q))
    set_records(0, incoming + descended, own_proxies)

    def far_leaf(leaf, carry):
        xyz = targets_xyz[leaf]
        rows = rows_of(
            apply_points(
                [xyz[axis : axis + 1] for axis in range(3)],
                loader(scratch_rec, 0),
                turns,
                zeros_acc(F),
            )
        )
        near[leaf] = near[leaf] * (1.0 / math.sqrt(LEAF * PAIRS_LEAF)) + rows * (
            RADIUS_BOX / math.sqrt(Q)
        )
        return carry

    lax.fori_loop(0, LEAVES, far_leaf, 0)
    sources = sources_ref[...]
    result = 0.5 * sources + jnp.concatenate([near[leaf] for leaf in range(LEAVES)], axis=1)
    result_ref[...] = result

    s_re, s_im = sources[:F], sources[F:]
    r_re, r_im = result[:F], result[F:]
    real_sum = jnp.sum(s_re * r_re + s_im * r_im, axis=1, keepdims=True)
    imag_sum = jnp.sum(s_re * r_im - s_im * r_re, axis=1, keepdims=True)
    squares = jnp.sum(s_re * s_re + s_im * s_im, axis=1, keepdims=True)
    lane = lax.broadcasted_iota(jnp.int32, (F, 128), 1)
    mine = jnp.where(
        lane == 0, real_sum, jnp.where(lane == 1, imag_sum, jnp.where(lane == 2, squares, 0.0))
    )
    sums_send[...] = mine
    sums[me] = mine

    def send_sums(step, carry):
        send_to(sums_send, sums.at[me], sums_send_sem, sums_recv_sem, (me + step) % count)
        return carry

    lax.fori_loop(1, count, send_sums, 0)

    for halo in halos:
        halo.wait_send()
    wait_bytes(gathered, count - 1, gather_send_sem)
    wait_bytes(contributions, GROUP - 1, up_send_sem)
    if groups > 1:
        wait_bytes(group_multipoles, groups - 1, across_send_sem)
    wait_bytes(group_locals, GROUP - 1, down_send_sem)
    wait_bytes(sums, count - 1, sums_recv_sem)
    total = jnp.sum(sums[...], axis=0).T
    rayleigh_ref[...] = total[0:2, :] / (total[2:3, :] + 1e-06)
    wait_bytes(sums, count - 1, sums_send_sem)


def on_device(
    sec_size,
    dev_size,
    sources,
    positions,
    weights,
    wavenumbers,
    directions,
    box_centers,
    group_centers,
    near_pairs,
    pair_counts,
    box_lists,
    group_lists,
):
    count = sec_size * dev_size
    groups = count // GROUP
    smem = pl.BlockSpec(memory_space=pltpu.SMEM)
    vmem = pl.BlockSpec(memory_space=pltpu.VMEM)
    f32 = jnp.float32
    result, rayleigh = pl.pallas_call(
        functools.partial(kernel, sec_size, dev_size, groups),
        out_shape=(
            jax.ShapeDtypeStruct((ROWS, P_DEV), f32),
            jax.ShapeDtypeStruct((2, F), f32),
        ),
        in_specs=[smem] * 7 + [vmem] * 4,
        out_specs=(vmem, vmem),
        scratch_shapes=[
            pltpu.VMEM((3, REC, P_DEV), f32),
            pltpu.VMEM((3 * LEAVES, LEAF, REC), f32),
            pltpu.VMEM((LEAVES, 8, LEAF), f32),
            pltpu.VMEM((Q, 8), f32),
            pltpu.VMEM((1, Q, REC), f32),
            pltpu.VMEM((ROWS, Q), f32),
            pltpu.VMEM((count, ROWS, Q), f32),
            pltpu.VMEM((F, 8, Q), f32),
            pltpu.VMEM((GROUP, 8, Q), f32),
            pltpu.VMEM((8, Q), f32),
            pltpu.VMEM((groups, 8, Q), f32),
            pltpu.VMEM((8, Q), f32),
            pltpu.VMEM((GROUP, 8, Q), f32),
            pltpu.VMEM((LEAVES, ROWS, LEAF), f32),
            pltpu.VMEM((ROWS, Q), f32),
            pltpu.VMEM((F, 128), f32),
            pltpu.VMEM((count, F, 128), f32),
            pltpu.SemaphoreType.DMA((2,)),
            pltpu.SemaphoreType.DMA((2,)),
        ]
        + [pltpu.SemaphoreType.DMA] * 10,
        compiler_params=pltpu.CompilerParams(
            collective_id=0, has_side_effects=True, vmem_limit_bytes=32 * 1024 * 1024
        ),
        name="bem_matvec",
    )(
        wavenumbers,
        box_centers,
        group_centers,
        near_pairs[0],
        pair_counts,
        box_lists,
        group_lists,
        sources.reshape(ROWS, P_DEV),
        positions,
        weights[None, :],
        directions,
    )
    return result.reshape(2, F, P_DEV), rayleigh


def solution(mesh):
    in_specs = (
        P(None, None, ("sec", "dev")),
        P(None, ("sec", "dev")),
        P(("sec", "dev")),
        P(),
        P(),
        P(),
        P(),
        P(("sec", "dev"), None, None),
        P(("sec", "dev")),
        P(("sec", "dev"), None),
        P(),
    )
    out_specs = (P(None, None, ("sec", "dev")), P())
    return jax.shard_map(
        functools.partial(on_device, mesh.shape["sec"], mesh.shape["dev"]),
        mesh=mesh,
        in_specs=in_specs,
        out_specs=out_specs,
        check_vma=False,
    )
```

```python
import functools
import math

import jax
import jax.numpy as jnp
from jax import lax
from jax.experimental import pallas as pl
from jax.experimental.pallas import tpu as pltpu
from jax.sharding import PartitionSpec as P

LEAF = 128
LEAVES = 2
F = 8
Q = 128
PAIRS_LEAF = 5
ML1 = 4
ML2 = 2
GROUP = 8
P_DEV = 256
PAIRS_MAX = 10

SOFT = 0.1
RADIUS_BOX = 1.0 + 0.5 * LEAVES
RADIUS_GROUP = 2.0 * RADIUS_BOX
ROWS = 2 * F
REC = 24
BLOCK = 32
ROUNDER = 12582912.0

COS = (
    0.9999992216144897,
    -19.738982519159087,
    64.9287266658944,
    -85.27239730229532,
    58.794039342441934,
    -21.076782244925596,
)
SIN = (
    6.283055797987737,
    -41.33121426662637,
    81.36681462152343,
    -74.47800045497374,
    32.7813926131928,
)
MESH = pl.DeviceIdType.MESH


def horner(coefficients, z):
    total = coefficients[-1]
    for coefficient in coefficients[-2::-1]:
        total = total * z + coefficient
    return total


def geometry(target, cols):
    squared = SOFT * SOFT
    for axis in range(3):
        offset = target[axis] - cols[:, ROWS + axis : ROWS + axis + 1]
        squared = squared + offset * offset
    inverse = lax.rsqrt(squared)
    distance = squared * inverse
    distance = distance + (0.5 * inverse) * (squared - distance * distance)
    return distance, inverse


def point_terms(distance, inverse, turns, real, imag):
    phase = distance * turns
    phase = phase - ((phase + ROUNDER) - ROUNDER)
    z = phase * phase
    cosine = inverse * horner(COS, z)
    sine = (inverse * phase) * horner(SIN, z)
    return cosine * real - sine * imag, cosine * imag + sine * real


def fold(block):
    return block.reshape(block.shape[0] // 8, 8, block.shape[1]).sum(0)


def apply_points(geo, target, load, turns, add):
    blocks = range(LEAF // BLOCK)
    for block in blocks:
        distance, inverse = geometry(target, load(block))
        geo[0, pl.ds(block * BLOCK, BLOCK), :] = distance
        geo[1, pl.ds(block * BLOCK, BLOCK), :] = inverse
    for f in range(F):
        total_re, total_im = 0.0, 0.0
        for block in blocks:
            cols = load(block)
            re, im = point_terms(
                geo[0, pl.ds(block * BLOCK, BLOCK), :],
                geo[1, pl.ds(block * BLOCK, BLOCK), :],
                turns[f],
                cols[:, f : f + 1],
                cols[:, F + f : F + f + 1],
            )
            total_re = total_re + fold(re)
            total_im = total_im + fold(im)
        add(f, total_re)
        add(F + f, total_im)


def adder(ref, first=False):
    def add(row, term):
        ref[row] = term if first else ref[row] + term

    return add


def rows_of(acc):
    return jnp.sum(acc, axis=1)


def wrapped(index, size):
    return jnp.where(index >= size, index - size, index)


def kernel(
    sec_size,
    dev_size,
    groups,
    wave_hbm,
    centers_hbm,
    group_centers_hbm,
    pairs_hbm,
    counts_hbm,
    lists_hbm,
    group_lists_hbm,
    sources_hbm,
    positions_hbm,
    weights_hbm,
    directions_hbm,
    result_ref,
    rayleigh_ref,
    wave_ref,
    centers_ref,
    group_centers_ref,
    pairs_ref,
    counts_ref,
    lists_ref,
    group_lists_ref,
    sources_ref,
    positions_ref,
    weights_ref,
    directions_ref,
    geo,
    acc,
    window,
    records,
    targets_xyz,
    scratch_rec,
    gathered,
    contribution,
    contributions,
    group_send,
    group_multipoles,
    local_send,
    group_locals,
    near,
    sums_send,
    sums,
    totals_send,
    totals,
    operand_sem,
    halo_send_sem,
    halo_recv_sem,
    wide_send_sem,
    wide_recv_sem,
    gather_send_sem,
    gather_recv_sem,
    up_send_sem,
    up_recv_sem,
    across_send_sem,
    across_recv_sem,
    down_send_sem,
    down_recv_sem,
    sums_send_sem,
    sums_recv_sem,
    totals_send_sem,
    totals_recv_sem,
):
    count = sec_size * dev_size
    sec, dev = lax.axis_index("sec"), lax.axis_index("dev")
    me = sec * dev_size + dev
    per_row = dev_size // GROUP
    group = me // GROUP
    member = dev % GROUP
    first = dev - member
    mates = [wrapped(member + step, GROUP) for step in range(1, GROUP)]
    mate_places = [(sec, first + mate) for mate in mates]
    far_places = [
        (wrapped(sec + row, sec_size), wrapped(dev + column * GROUP, dev_size))
        for row in range(sec_size)
        for column in range(per_row)
        if row or column
    ]
    last, begin = dev == dev_size - 1, dev == 0
    after = (
        jnp.where(last, wrapped(sec + 1, sec_size), sec),
        jnp.where(last, 0, dev + 1),
    )
    before = (
        jnp.where(begin, wrapped(sec + sec_size - 1, sec_size), sec),
        jnp.where(begin, dev_size - 1, dev - 1),
    )

    operands = [
        pltpu.make_async_copy(src, dst, operand_sem.at[index])
        for index, (src, dst) in enumerate(
            (
                (sources_hbm, sources_ref),
                (weights_hbm, weights_ref),
                (positions_hbm, positions_ref),
                (directions_hbm, directions_ref),
                (wave_hbm, wave_ref),
                (centers_hbm, centers_ref),
                (group_centers_hbm, group_centers_ref),
                (pairs_hbm, pairs_ref),
                (counts_hbm, counts_ref),
                (lists_hbm, lists_ref),
                (group_lists_hbm, group_lists_ref),
            )
        )
    ]
    for operand in operands:
        operand.start()

    barrier = pltpu.get_barrier_semaphore()
    partners = mate_places + far_places + [after, before]
    for partner in partners:
        pl.semaphore_signal(barrier, inc=1, device_id=partner, device_id_type=MESH)
    for operand in operands:
        operand.wait()

    turns = [wave_ref[f] * (0.5 / math.pi) for f in range(F)]

    weighted = sources_ref[...] * weights_ref[...]
    own_rows = jnp.concatenate(
        [weighted, positions_ref[...], jnp.zeros((REC - ROWS - 3, P_DEV), jnp.float32)], axis=0
    )
    window[1] = own_rows
    for leaf in range(LEAVES):
        part = own_rows[:, leaf * LEAF : (leaf + 1) * LEAF]
        records[LEAVES + leaf] = part.T
        targets_xyz[leaf] = part[ROWS : ROWS + 8]
    directions = directions_ref[...]

    def proxies(centers, index, radius):
        return [centers[axis, index] + radius * directions[axis : axis + 1] for axis in range(3)]

    own_proxies = proxies(centers_ref, me, RADIUS_BOX)
    parent_proxies = proxies(group_centers_ref, group, RADIUS_GROUP)
    row_padding = jnp.zeros((REC - ROWS - 3, Q), jnp.float32)

    def set_records(slot, rows, xyz):
        scratch_rec[slot] = jnp.concatenate([rows, *xyz, row_padding], axis=0).T

    def loader(ref, index):
        return lambda block: ref[index, pl.ds(pl.multiple_of(block * BLOCK, BLOCK), BLOCK), :]

    acc[...] = jnp.zeros_like(acc)

    def outward_leaf(leaf, carry):
        apply_points(geo, own_proxies, loader(records, LEAVES + leaf), turns, adder(acc))
        return carry

    lax.fori_loop(0, LEAVES, outward_leaf, 0)
    own_multipole = rows_of(acc[...]) * (RADIUS_BOX / math.sqrt(P_DEV))
    gathered[member, group] = own_multipole

    pl.semaphore_wait(barrier, len(partners))

    halos = [
        pltpu.make_async_remote_copy(
            src_ref=window.at[1],
            dst_ref=window.at[slot],
            send_sem=halo_send_sem.at[way],
            recv_sem=halo_recv_sem.at[way],
            device_id=device,
            device_id_type=MESH,
        )
        for way, (slot, device) in enumerate(((0, after), (2, before)))
    ]
    for halo in halos:
        halo.start()

    def send_to(src, dst, send_sem, recv_sem, device):
        pltpu.make_async_remote_copy(
            src_ref=src,
            dst_ref=dst,
            send_sem=send_sem,
            recv_sem=recv_sem,
            device_id=device,
            device_id_type=MESH,
        ).start()

    def wait_bytes(ref, pieces, sem):
        part = ref.at[pl.ds(0, pieces)]
        pltpu.make_async_copy(part, part, sem).wait()

    own_slot = gathered.at[member, group]
    for device in far_places:
        send_to(own_slot, own_slot, wide_send_sem, wide_recv_sem, device)

    set_records(0, own_multipole, own_proxies)
    apply_points(geo, parent_proxies, loader(scratch_rec, 0), turns, adder(acc, True))
    terms = rows_of(acc[...]) * (RADIUS_GROUP / math.sqrt(GROUP * Q))
    padding = jnp.zeros((6, Q), jnp.float32)
    for f in range(F):
        contribution[f] = jnp.concatenate(
            [terms[f : f + 1], terms[F + f : F + f + 1], padding], axis=0
        )
    contributions[member] = contribution[member]
    for mate, device in zip(mates, mate_places):
        send_to(
            contribution.at[mate], contributions.at[member], up_send_sem, up_recv_sem, device
        )

    for way, halo in enumerate(halos):
        halo.wait_recv()
        slot = 2 * way
        inside = jnp.where(me > 0, 1.0, 0.0) if way == 0 else jnp.where(me < count - 1, 1.0, 0.0)
        rows = window[slot]
        rows = jnp.concatenate([rows[:ROWS] * inside, rows[ROWS:]], axis=0)
        for leaf in range(LEAVES):
            records[slot * LEAVES + leaf] = rows[:, leaf * LEAF : (leaf + 1) * LEAF].T
    near[...] = jnp.zeros_like(near)

    def near_pair(pair, carry):
        target = pairs_ref[0, 0, pair]
        anchor = pairs_ref[0, 1, pair]
        live = jnp.where(pair < counts_ref[0], 1.0, 0.0)
        xyz = targets_xyz[target]
        lives = [jnp.where(target == leaf, live, 0.0) for leaf in range(LEAVES)]

        def add(row, term):
            for leaf in range(LEAVES):
                near[leaf, row] += term * lives[leaf]

        apply_points(
            geo, [xyz[axis : axis + 1] for axis in range(3)], loader(records, anchor), turns, add
        )
        return carry

    first_half = PAIRS_MAX // 2
    lax.fori_loop(0, first_half, near_pair, 0)

    wait_bytes(contributions, GROUP - 1, up_recv_sem)
    total = contributions[0]
    for other in range(1, GROUP):
        total = total + contributions[other]
    group_send[...] = total
    group_multipoles[group] = total

    for device in far_places:
        send_to(
            group_send, group_multipoles.at[group], across_send_sem, across_recv_sem, device
        )

    if groups > 1:
        wait_bytes(gathered.at[0], groups - 1, wide_recv_sem)
    own_part = gathered.at[member]
    for device in mate_places:
        send_to(own_part, own_part, gather_send_sem, gather_recv_sem, device)

    lax.fori_loop(first_half, PAIRS_MAX, near_pair, 0)

    if groups > 1:
        wait_bytes(group_multipoles, groups - 1, across_recv_sem)
    my_turns = wave_ref[member] * (0.5 / math.pi)
    local_re, local_im = 0.0, 0.0
    for m in range(ML2):
        other = group_lists_ref[m, group]
        rows = group_multipoles[other]
        xyz = proxies(group_centers_ref, other, RADIUS_GROUP)
        cols = jnp.concatenate([rows, rows, *xyz, row_padding], axis=0).T
        for block in range(Q // BLOCK):
            part = cols[block * BLOCK : (block + 1) * BLOCK]
            distance, inverse = geometry(parent_proxies, part)
            re, im = point_terms(distance, inverse, my_turns, part[:, 0:1], part[:, 1:2])
            local_re = local_re + fold(re)
            local_im = local_im + fold(im)
    local_rows = [jnp.sum(part, axis=0, keepdims=True) for part in (local_re, local_im)]
    local = jnp.concatenate([*local_rows, padding], axis=0) * (
        RADIUS_GROUP / math.sqrt(ML2 * Q)
    )
    local_send[...] = local
    group_locals[member] = local

    for device in mate_places:
        send_to(local_send, group_locals.at[member], down_send_sem, down_recv_sem, device)

    wait_bytes(gathered, GROUP - 1, gather_recv_sem)
    acc[...] = jnp.zeros_like(acc)

    def list_box(m, carry):
        other = lists_ref[0, m]
        set_records(
            0, gathered[other % GROUP, other // GROUP], proxies(centers_ref, other, RADIUS_BOX)
        )
        apply_points(geo, own_proxies, loader(scratch_rec, 0), turns, adder(acc))
        return carry

    lax.fori_loop(0, ML1, list_box, 0)
    incoming = rows_of(acc[...]) * (RADIUS_BOX / math.sqrt(ML1 * Q))

    wait_bytes(group_locals, GROUP - 1, down_recv_sem)
    rows = jnp.concatenate(
        [group_locals[f][part : part + 1] for part in range(2) for f in range(F)], axis=0
    )
    set_records(0, rows, parent_proxies)
    apply_points(geo, own_proxies, loader(scratch_rec, 0), turns, adder(acc, True))
    descended = rows_of(acc[...]) * (RADIUS_GROUP / math.sqrt(Q))
    set_records(0, incoming + descended, own_proxies)

    def far_leaf(leaf, carry):
        xyz = targets_xyz[leaf]

        def add(row, term):
            near[leaf, row] = near[leaf, row] * (1.0 / math.sqrt(LEAF * PAIRS_LEAF)) + term * (
                RADIUS_BOX / math.sqrt(Q)
            )

        apply_points(
            geo, [xyz[axis : axis + 1] for axis in range(3)], loader(scratch_rec, 0), turns, add
        )
        return carry

    lax.fori_loop(0, LEAVES, far_leaf, 0)
    sources = sources_ref[...]
    result = 0.5 * sources + jnp.concatenate([rows_of(near[leaf]) for leaf in range(LEAVES)], axis=1)
    result_ref[...] = result

    s_re, s_im = sources[:F], sources[F:]
    r_re, r_im = result[:F], result[F:]
    real_sum = jnp.sum(s_re * r_re + s_im * r_im, axis=1, keepdims=True)
    imag_sum = jnp.sum(s_re * r_im - s_im * r_re, axis=1, keepdims=True)
    squares = jnp.sum(s_re * s_re + s_im * s_im, axis=1, keepdims=True)
    lane = lax.broadcasted_iota(jnp.int32, (F, 128), 1)
    mine = jnp.where(
        lane == 0, real_sum, jnp.where(lane == 1, imag_sum, jnp.where(lane == 2, squares, 0.0))
    )
    sums_send[...] = mine
    sums[member] = mine
    for device in mate_places:
        send_to(sums_send, sums.at[member], sums_send_sem, sums_recv_sem, device)

    for halo in halos:
        halo.wait_send()
    if groups > 1:
        wait_bytes(gathered.at[0], groups - 1, wide_send_sem)
        wait_bytes(group_multipoles, groups - 1, across_send_sem)
    wait_bytes(gathered, GROUP - 1, gather_send_sem)
    wait_bytes(contributions, GROUP - 1, up_send_sem)
    wait_bytes(group_locals, GROUP - 1, down_send_sem)

    wait_bytes(sums, GROUP - 1, sums_recv_sem)
    total = jnp.sum(sums[...], axis=0)
    totals_send[...] = total
    totals[group] = total
    for device in far_places:
        send_to(totals_send, totals.at[group], totals_send_sem, totals_recv_sem, device)
    wait_bytes(sums, GROUP - 1, sums_send_sem)
    if groups > 1:
        wait_bytes(totals, groups - 1, totals_recv_sem)
    total = jnp.sum(totals[...], axis=0).T
    rayleigh_ref[...] = total[0:2, :] / (total[2:3, :] + 1e-06)
    if groups > 1:
        wait_bytes(totals, groups - 1, totals_send_sem)


def on_device(
    sec_size,
    dev_size,
    sources,
    positions,
    weights,
    wavenumbers,
    directions,
    box_centers,
    group_centers,
    near_pairs,
    pair_counts,
    box_lists,
    group_lists,
):
    count = sec_size * dev_size
    groups = count // GROUP
    hbm = pl.BlockSpec(memory_space=pltpu.HBM)
    vmem = pl.BlockSpec(memory_space=pltpu.VMEM)
    f32 = jnp.float32
    result, rayleigh = pl.pallas_call(
        functools.partial(kernel, sec_size, dev_size, groups),
        out_shape=(
            jax.ShapeDtypeStruct((ROWS, P_DEV), f32),
            jax.ShapeDtypeStruct((2, F), f32),
        ),
        in_specs=[hbm] * 11,
        out_specs=(vmem, vmem),
        scratch_shapes=[
            pltpu.SMEM((F,), f32),
            pltpu.SMEM((3, count), f32),
            pltpu.SMEM((3, groups), f32),
            pltpu.SMEM((1, 2, PAIRS_MAX), jnp.int32),
            pltpu.SMEM((1,), jnp.int32),
            pltpu.SMEM((1, ML1), jnp.int32),
            pltpu.SMEM((ML2, groups), jnp.int32),
            pltpu.VMEM((ROWS, P_DEV), f32),
            pltpu.VMEM((3, P_DEV), f32),
            pltpu.VMEM((1, P_DEV), f32),
            pltpu.VMEM((3, Q), f32),
            pltpu.VMEM((2, LEAF, 128), f32),
            pltpu.VMEM((ROWS, 8, 128), f32),
            pltpu.VMEM((3, REC, P_DEV), f32),
            pltpu.VMEM((3 * LEAVES, LEAF, REC), f32),
            pltpu.VMEM((LEAVES, 8, LEAF), f32),
            pltpu.VMEM((1, Q, REC), f32),
            pltpu.VMEM((GROUP, groups, ROWS, Q), f32),
            pltpu.VMEM((F, 8, Q), f32),
            pltpu.VMEM((GROUP, 8, Q), f32),
            pltpu.VMEM((8, Q), f32),
            pltpu.VMEM((groups, 8, Q), f32),
            pltpu.VMEM((8, Q), f32),
            pltpu.VMEM((GROUP, 8, Q), f32),
            pltpu.VMEM((LEAVES, ROWS, 8, LEAF), f32),
            pltpu.VMEM((F, 128), f32),
            pltpu.VMEM((GROUP, F, 128), f32),
            pltpu.VMEM((F, 128), f32),
            pltpu.VMEM((groups, F, 128), f32),
            pltpu.SemaphoreType.DMA((11,)),
            pltpu.SemaphoreType.DMA((2,)),
            pltpu.SemaphoreType.DMA((2,)),
        ]
        + [pltpu.SemaphoreType.DMA] * 14,
        compiler_params=pltpu.CompilerParams(
            collective_id=0, has_side_effects=True, vmem_limit_bytes=32 * 1024 * 1024
        ),
        name="bem_matvec",
    )(
        wavenumbers,
        box_centers,
        group_centers,
        near_pairs,
        pair_counts,
        box_lists,
        group_lists.T,
        sources.reshape(ROWS, P_DEV),
        positions,
        weights[None, :],
        directions,
    )
    return result.reshape(2, F, P_DEV), rayleigh


def solution(mesh):
    in_specs = (
        P(None, None, ("sec", "dev")),
        P(None, ("sec", "dev")),
        P(("sec", "dev")),
        P(),
        P(),
        P(),
        P(),
        P(("sec", "dev"), None, None),
        P(("sec", "dev")),
        P(("sec", "dev"), None),
        P(),
    )
    out_specs = (P(None, None, ("sec", "dev")), P())
    return jax.shard_map(
        functools.partial(on_device, mesh.shape["sec"], mesh.shape["dev"]),
        mesh=mesh,
        in_specs=in_specs,
        out_specs=out_specs,
        check_vma=False,
    )
```

```python
import functools
import math

import jax
import jax.numpy as jnp
from jax import lax
from jax.experimental import pallas as pl
from jax.experimental.pallas import tpu as pltpu
from jax.sharding import PartitionSpec as P

LEAF = 128
LEAVES = 2
F = 8
Q = 128
PAIRS_LEAF = 5
ML1 = 4
ML2 = 2
GROUP = 8
P_DEV = 256
PAIRS_MAX = 10

SOFT = 0.1
RADIUS_BOX = 1.0 + 0.5 * LEAVES
RADIUS_GROUP = 2.0 * RADIUS_BOX
ROWS = 2 * F
REC = 24
SPLIT = 3 * ROWS
BLOCK = 32
ROUNDER = 12582912.0

COS = (
    0.9999992216144897,
    -19.738982519159087,
    64.9287266658944,
    -85.27239730229532,
    58.794039342441934,
    -21.076782244925596,
)
SIN = (
    6.283055797987737,
    -41.33121426662637,
    81.36681462152343,
    -74.47800045497374,
    32.7813926131928,
)
MESH = pl.DeviceIdType.MESH


def horner(coefficients, z):
    total = coefficients[-1]
    for coefficient in coefficients[-2::-1]:
        total = total * z + coefficient
    return total


def geometry(target, cols):
    squared = SOFT * SOFT
    for axis in range(3):
        offset = target[axis] - cols[:, axis : axis + 1]
        squared = squared + offset * offset
    inverse = lax.rsqrt(squared)
    distance = squared * inverse
    distance = distance + (0.5 * inverse) * (squared - distance * distance)
    return distance, inverse


def point_terms(distance, inverse, turns, real, imag):
    phase = distance * turns
    phase = phase - ((phase + ROUNDER) - ROUNDER)
    z = phase * phase
    cosine = inverse * horner(COS, z)
    sine = (inverse * phase) * horner(SIN, z)
    return cosine * real - sine * imag, cosine * imag + sine * real


def fold(block):
    return block.reshape(block.shape[0] // 8, 8, block.shape[1]).sum(0)


def apply_points(geo, spread, target, record, turns, add):
    values, xyz = record
    blocks = range(LEAF // BLOCK)
    for block in blocks:
        distance, inverse = geometry(target, xyz(block))
        geo[0, pl.ds(block * BLOCK, BLOCK), :] = distance
        geo[1, pl.ds(block * BLOCK, BLOCK), :] = inverse
    for f in range(F):
        wide = jnp.dot(
            values(), spread[:, f * 256 : (f + 1) * 256], preferred_element_type=jnp.float32
        )
        total_re, total_im = 0.0, 0.0
        for block in blocks:
            part = wide[block * BLOCK : (block + 1) * BLOCK]
            re, im = point_terms(
                geo[0, pl.ds(block * BLOCK, BLOCK), :],
                geo[1, pl.ds(block * BLOCK, BLOCK), :],
                turns[f],
                part[:, :128],
                part[:, 128:],
            )
            total_re = total_re + fold(re)
            total_im = total_im + fold(im)
        add(f, total_re)
        add(F + f, total_im)


def record_columns(rows):
    values = rows[:ROWS]
    high = values.astype(jnp.bfloat16).astype(jnp.float32)
    rest = values - high
    middle = rest.astype(jnp.bfloat16).astype(jnp.float32)
    low = rest - middle
    cols = jnp.concatenate([high, middle, low, rows[ROWS:]], axis=0).T
    return cols[:, :SPLIT].astype(jnp.bfloat16), cols[:, SPLIT:]


def adder(ref, first=False):
    def add(row, term):
        ref[row] = term if first else ref[row] + term

    return add


def rows_of(acc):
    return jnp.sum(acc, axis=1)


def wrapped(index, size):
    return jnp.where(index >= size, index - size, index)


def kernel(
    sec_size,
    dev_size,
    groups,
    wave_hbm,
    centers_hbm,
    group_centers_hbm,
    pairs_hbm,
    counts_hbm,
    lists_hbm,
    group_lists_hbm,
    sources_hbm,
    positions_hbm,
    weights_hbm,
    directions_hbm,
    result_ref,
    rayleigh_ref,
    wave_ref,
    centers_ref,
    group_centers_ref,
    pairs_ref,
    counts_ref,
    lists_ref,
    group_lists_ref,
    sources_ref,
    positions_ref,
    weights_ref,
    directions_ref,
    geo,
    spread,
    acc,
    window,
    records,
    records_xyz,
    targets_xyz,
    scratch_rec,
    scratch_xyz,
    gathered,
    contribution,
    contributions,
    group_send,
    group_multipoles,
    local_send,
    group_locals,
    near,
    sums_send,
    sums,
    totals_send,
    totals,
    operand_sem,
    halo_send_sem,
    halo_recv_sem,
    wide_send_sem,
    wide_recv_sem,
    gather_send_sem,
    gather_recv_sem,
    up_send_sem,
    up_recv_sem,
    across_send_sem,
    across_recv_sem,
    down_send_sem,
    down_recv_sem,
    sums_send_sem,
    sums_recv_sem,
    totals_send_sem,
    totals_recv_sem,
):
    count = sec_size * dev_size
    sec, dev = lax.axis_index("sec"), lax.axis_index("dev")
    me = sec * dev_size + dev
    per_row = dev_size // GROUP
    group = me // GROUP
    member = dev % GROUP
    first = dev - member
    mates = [wrapped(member + step, GROUP) for step in range(1, GROUP)]
    mate_places = [(sec, first + mate) for mate in mates]
    far_places = [
        (wrapped(sec + row, sec_size), wrapped(dev + column * GROUP, dev_size))
        for row in range(sec_size)
        for column in range(per_row)
        if row or column
    ]
    last, begin = dev == dev_size - 1, dev == 0
    after = (
        jnp.where(last, wrapped(sec + 1, sec_size), sec),
        jnp.where(last, 0, dev + 1),
    )
    before = (
        jnp.where(begin, wrapped(sec + sec_size - 1, sec_size), sec),
        jnp.where(begin, dev_size - 1, dev - 1),
    )

    operands = [
        pltpu.make_async_copy(src, dst, operand_sem.at[index])
        for index, (src, dst) in enumerate(
            (
                (sources_hbm, sources_ref),
                (weights_hbm, weights_ref),
                (positions_hbm, positions_ref),
                (directions_hbm, directions_ref),
                (wave_hbm, wave_ref),
                (centers_hbm, centers_ref),
                (group_centers_hbm, group_centers_ref),
                (pairs_hbm, pairs_ref),
                (counts_hbm, counts_ref),
                (lists_hbm, lists_ref),
                (group_lists_hbm, group_lists_ref),
            )
        )
    ]
    for operand in operands:
        operand.start()

    barrier = pltpu.get_barrier_semaphore()
    partners = mate_places + far_places + [after, before]
    for partner in partners:
        pl.semaphore_signal(barrier, inc=1, device_id=partner, device_id_type=MESH)
    row = lax.broadcasted_iota(jnp.int32, (SPLIT, 2 * 128 * F), 0) % ROWS
    column = lax.broadcasted_iota(jnp.int32, (SPLIT, 2 * 128 * F), 1) // 128
    spread[...] = jnp.where(row == column // 2 + F * (column % 2), 1.0, 0.0).astype(jnp.bfloat16)

    for operand in operands:
        operand.wait()

    turns = [wave_ref[f] * (0.5 / math.pi) for f in range(F)]

    weighted = sources_ref[...] * weights_ref[...]
    own_rows = jnp.concatenate(
        [weighted, positions_ref[...], jnp.zeros((REC - ROWS - 3, P_DEV), jnp.float32)], axis=0
    )
    window[1] = own_rows
    for leaf in range(LEAVES):
        part = own_rows[:, leaf * LEAF : (leaf + 1) * LEAF]
        records[LEAVES + leaf], records_xyz[LEAVES + leaf] = record_columns(part)
        targets_xyz[leaf] = part[ROWS : ROWS + 8]
    directions = directions_ref[...]

    def proxies(centers, index, radius):
        return [centers[axis, index] + radius * directions[axis : axis + 1] for axis in range(3)]

    own_proxies = proxies(centers_ref, me, RADIUS_BOX)
    parent_proxies = proxies(group_centers_ref, group, RADIUS_GROUP)
    row_padding = jnp.zeros((REC - ROWS - 3, Q), jnp.float32)

    def set_records(slot, rows, xyz):
        scratch_rec[slot], scratch_xyz[slot] = record_columns(
            jnp.concatenate([rows, *xyz, row_padding], axis=0)
        )

    def loader(ref, index):
        xyz = records_xyz if ref is records else scratch_xyz
        return (
            lambda: ref[index],
            lambda block: xyz[index, pl.ds(block * BLOCK, BLOCK), :],
        )

    acc[...] = jnp.zeros_like(acc)

    def outward_leaf(leaf, carry):
        apply_points(geo, spread, own_proxies, loader(records, LEAVES + leaf), turns, adder(acc))
        return carry

    lax.fori_loop(0, LEAVES, outward_leaf, 0)
    own_multipole = rows_of(acc[...]) * (RADIUS_BOX / math.sqrt(P_DEV))
    gathered[member, group] = own_multipole

    pl.semaphore_wait(barrier, len(partners))

    halos = [
        pltpu.make_async_remote_copy(
            src_ref=window.at[1],
            dst_ref=window.at[slot],
            send_sem=halo_send_sem.at[way],
            recv_sem=halo_recv_sem.at[way],
            device_id=device,
            device_id_type=MESH,
        )
        for way, (slot, device) in enumerate(((0, after), (2, before)))
    ]
    for halo in halos:
        halo.start()

    def send_to(src, dst, send_sem, recv_sem, device):
        pltpu.make_async_remote_copy(
            src_ref=src,
            dst_ref=dst,
            send_sem=send_sem,
            recv_sem=recv_sem,
            device_id=device,
            device_id_type=MESH,
        ).start()

    def wait_bytes(ref, pieces, sem):
        part = ref.at[pl.ds(0, pieces)]
        pltpu.make_async_copy(part, part, sem).wait()

    own_slot = gathered.at[member, group]
    for device in far_places:
        send_to(own_slot, own_slot, wide_send_sem, wide_recv_sem, device)

    set_records(0, own_multipole, own_proxies)
    apply_points(geo, spread, parent_proxies, loader(scratch_rec, 0), turns, adder(acc, True))
    terms = rows_of(acc[...]) * (RADIUS_GROUP / math.sqrt(GROUP * Q))
    padding = jnp.zeros((6, Q), jnp.float32)
    for f in range(F):
        contribution[f] = jnp.concatenate(
            [terms[f : f + 1], terms[F + f : F + f + 1], padding], axis=0
        )
    contributions[member] = contribution[member]
    for mate, device in zip(mates, mate_places):
        send_to(
            contribution.at[mate], contributions.at[member], up_send_sem, up_recv_sem, device
        )

    for way, halo in enumerate(halos):
        halo.wait_recv()
        slot = 2 * way
        inside = jnp.where(me > 0, 1.0, 0.0) if way == 0 else jnp.where(me < count - 1, 1.0, 0.0)
        rows = window[slot]
        rows = jnp.concatenate([rows[:ROWS] * inside, rows[ROWS:]], axis=0)
        for leaf in range(LEAVES):
            index = slot * LEAVES + leaf
            records[index], records_xyz[index] = record_columns(
                rows[:, leaf * LEAF : (leaf + 1) * LEAF]
            )
    near[...] = jnp.zeros_like(near)

    def near_pair(pair, carry):
        target = pairs_ref[0, 0, pair]
        anchor = pairs_ref[0, 1, pair]
        live = jnp.where(pair < counts_ref[0], 1.0, 0.0)
        xyz = targets_xyz[target]
        lives = [jnp.where(target == leaf, live, 0.0) for leaf in range(LEAVES)]

        def add(row, term):
            for leaf in range(LEAVES):
                near[leaf, row] += term * lives[leaf]

        apply_points(
            geo, spread, [xyz[axis : axis + 1] for axis in range(3)], loader(records, anchor), turns, add
        )
        return carry

    first_half = PAIRS_MAX // 2
    lax.fori_loop(0, first_half, near_pair, 0)

    wait_bytes(contributions, GROUP - 1, up_recv_sem)
    total = contributions[0]
    for other in range(1, GROUP):
        total = total + contributions[other]
    group_send[...] = total
    group_multipoles[group] = total

    for device in far_places:
        send_to(
            group_send, group_multipoles.at[group], across_send_sem, across_recv_sem, device
        )

    if groups > 1:
        wait_bytes(gathered.at[0], groups - 1, wide_recv_sem)
    own_part = gathered.at[member]
    for device in mate_places:
        send_to(own_part, own_part, gather_send_sem, gather_recv_sem, device)

    lax.fori_loop(first_half, PAIRS_MAX, near_pair, 0)

    if groups > 1:
        wait_bytes(group_multipoles, groups - 1, across_recv_sem)
    my_turns = wave_ref[member] * (0.5 / math.pi)
    local_re, local_im = 0.0, 0.0
    for m in range(ML2):
        other = group_lists_ref[m, group]
        rows = group_multipoles[other]
        xyz = proxies(group_centers_ref, other, RADIUS_GROUP)
        cols = jnp.concatenate([rows, *xyz, row_padding], axis=0).T
        for block in range(Q // BLOCK):
            part = cols[block * BLOCK : (block + 1) * BLOCK]
            distance, inverse = geometry(parent_proxies, part[:, 8:16])
            re, im = point_terms(distance, inverse, my_turns, part[:, 0:1], part[:, 1:2])
            local_re = local_re + fold(re)
            local_im = local_im + fold(im)
    local_rows = [jnp.sum(part, axis=0, keepdims=True) for part in (local_re, local_im)]
    local = jnp.concatenate([*local_rows, padding], axis=0) * (
        RADIUS_GROUP / math.sqrt(ML2 * Q)
    )
    local_send[...] = local
    group_locals[member] = local

    for device in mate_places:
        send_to(local_send, group_locals.at[member], down_send_sem, down_recv_sem, device)

    wait_bytes(gathered, GROUP - 1, gather_recv_sem)
    acc[...] = jnp.zeros_like(acc)

    def list_box(m, carry):
        other = lists_ref[0, m]
        set_records(
            0, gathered[other % GROUP, other // GROUP], proxies(centers_ref, other, RADIUS_BOX)
        )
        apply_points(geo, spread, own_proxies, loader(scratch_rec, 0), turns, adder(acc))
        return carry

    lax.fori_loop(0, ML1, list_box, 0)
    incoming = rows_of(acc[...]) * (RADIUS_BOX / math.sqrt(ML1 * Q))

    wait_bytes(group_locals, GROUP - 1, down_recv_sem)
    rows = jnp.concatenate(
        [group_locals[f][part : part + 1] for part in range(2) for f in range(F)], axis=0
    )
    set_records(0, rows, parent_proxies)
    apply_points(geo, spread, own_proxies, loader(scratch_rec, 0), turns, adder(acc, True))
    descended = rows_of(acc[...]) * (RADIUS_GROUP / math.sqrt(Q))
    set_records(0, incoming + descended, own_proxies)

    def far_leaf(leaf, carry):
        xyz = targets_xyz[leaf]

        def add(row, term):
            near[leaf, row] = near[leaf, row] * (1.0 / math.sqrt(LEAF * PAIRS_LEAF)) + term * (
                RADIUS_BOX / math.sqrt(Q)
            )

        apply_points(
            geo, spread, [xyz[axis : axis + 1] for axis in range(3)], loader(scratch_rec, 0), turns, add
        )
        return carry

    lax.fori_loop(0, LEAVES, far_leaf, 0)
    sources = sources_ref[...]
    result = 0.5 * sources + jnp.concatenate([rows_of(near[leaf]) for leaf in range(LEAVES)], axis=1)
    result_ref[...] = result

    s_re, s_im = sources[:F], sources[F:]
    r_re, r_im = result[:F], result[F:]
    real_sum = jnp.sum(s_re * r_re + s_im * r_im, axis=1, keepdims=True)
    imag_sum = jnp.sum(s_re * r_im - s_im * r_re, axis=1, keepdims=True)
    squares = jnp.sum(s_re * s_re + s_im * s_im, axis=1, keepdims=True)
    lane = lax.broadcasted_iota(jnp.int32, (F, 128), 1)
    mine = jnp.where(
        lane == 0, real_sum, jnp.where(lane == 1, imag_sum, jnp.where(lane == 2, squares, 0.0))
    )
    sums_send[...] = mine
    sums[member] = mine
    for device in mate_places:
        send_to(sums_send, sums.at[member], sums_send_sem, sums_recv_sem, device)

    for halo in halos:
        halo.wait_send()
    if groups > 1:
        wait_bytes(gathered.at[0], groups - 1, wide_send_sem)
        wait_bytes(group_multipoles, groups - 1, across_send_sem)
    wait_bytes(gathered, GROUP - 1, gather_send_sem)
    wait_bytes(contributions, GROUP - 1, up_send_sem)
    wait_bytes(group_locals, GROUP - 1, down_send_sem)

    wait_bytes(sums, GROUP - 1, sums_recv_sem)
    total = jnp.sum(sums[...], axis=0)
    totals_send[...] = total
    totals[group] = total
    for device in far_places:
        send_to(totals_send, totals.at[group], totals_send_sem, totals_recv_sem, device)
    wait_bytes(sums, GROUP - 1, sums_send_sem)
    if groups > 1:
        wait_bytes(totals, groups - 1, totals_recv_sem)
    total = jnp.sum(totals[...], axis=0).T
    rayleigh_ref[...] = total[0:2, :] / (total[2:3, :] + 1e-06)
    if groups > 1:
        wait_bytes(totals, groups - 1, totals_send_sem)


def on_device(
    sec_size,
    dev_size,
    sources,
    positions,
    weights,
    wavenumbers,
    directions,
    box_centers,
    group_centers,
    near_pairs,
    pair_counts,
    box_lists,
    group_lists,
):
    count = sec_size * dev_size
    groups = count // GROUP
    hbm = pl.BlockSpec(memory_space=pltpu.HBM)
    vmem = pl.BlockSpec(memory_space=pltpu.VMEM)
    f32 = jnp.float32
    result, rayleigh = pl.pallas_call(
        functools.partial(kernel, sec_size, dev_size, groups),
        out_shape=(
            jax.ShapeDtypeStruct((ROWS, P_DEV), f32),
            jax.ShapeDtypeStruct((2, F), f32),
        ),
        in_specs=[hbm] * 11,
        out_specs=(vmem, vmem),
        scratch_shapes=[
            pltpu.SMEM((F,), f32),
            pltpu.SMEM((3, count), f32),
            pltpu.SMEM((3, groups), f32),
            pltpu.SMEM((1, 2, PAIRS_MAX), jnp.int32),
            pltpu.SMEM((1,), jnp.int32),
            pltpu.SMEM((1, ML1), jnp.int32),
            pltpu.SMEM((ML2, groups), jnp.int32),
            pltpu.VMEM((ROWS, P_DEV), f32),
            pltpu.VMEM((3, P_DEV), f32),
            pltpu.VMEM((1, P_DEV), f32),
            pltpu.VMEM((3, Q), f32),
            pltpu.VMEM((2, LEAF, 128), f32),
            pltpu.VMEM((SPLIT, 2 * 128 * F), jnp.bfloat16),
            pltpu.VMEM((ROWS, 8, 128), f32),
            pltpu.VMEM((3, REC, P_DEV), f32),
            pltpu.VMEM((3 * LEAVES, LEAF, SPLIT), jnp.bfloat16),
            pltpu.VMEM((3 * LEAVES, LEAF, REC - ROWS), f32),
            pltpu.VMEM((LEAVES, 8, LEAF), f32),
            pltpu.VMEM((1, Q, SPLIT), jnp.bfloat16),
            pltpu.VMEM((1, Q, REC - ROWS), f32),
            pltpu.VMEM((GROUP, groups, ROWS, Q), f32),
            pltpu.VMEM((F, 8, Q), f32),
            pltpu.VMEM((GROUP, 8, Q), f32),
            pltpu.VMEM((8, Q), f32),
            pltpu.VMEM((groups, 8, Q), f32),
            pltpu.VMEM((8, Q), f32),
            pltpu.VMEM((GROUP, 8, Q), f32),
            pltpu.VMEM((LEAVES, ROWS, 8, LEAF), f32),
            pltpu.VMEM((F, 128), f32),
            pltpu.VMEM((GROUP, F, 128), f32),
            pltpu.VMEM((F, 128), f32),
            pltpu.VMEM((groups, F, 128), f32),
            pltpu.SemaphoreType.DMA((11,)),
            pltpu.SemaphoreType.DMA((2,)),
            pltpu.SemaphoreType.DMA((2,)),
        ]
        + [pltpu.SemaphoreType.DMA] * 14,
        compiler_params=pltpu.CompilerParams(
            collective_id=0, has_side_effects=True, vmem_limit_bytes=63 * 1024 * 1024
        ),
        name="bem_matvec",
    )(
        wavenumbers,
        box_centers,
        group_centers,
        near_pairs,
        pair_counts,
        box_lists,
        group_lists.T,
        sources.reshape(ROWS, P_DEV),
        positions,
        weights[None, :],
        directions,
    )
    return result.reshape(2, F, P_DEV), rayleigh


def solution(mesh):
    in_specs = (
        P(None, None, ("sec", "dev")),
        P(None, ("sec", "dev")),
        P(("sec", "dev")),
        P(),
        P(),
        P(),
        P(),
        P(("sec", "dev"), None, None),
        P(("sec", "dev")),
        P(("sec", "dev"), None),
        P(),
    )
    out_specs = (P(None, None, ("sec", "dev")), P())
    return jax.shard_map(
        functools.partial(on_device, mesh.shape["sec"], mesh.shape["dev"]),
        mesh=mesh,
        in_specs=in_specs,
        out_specs=out_specs,
        check_vma=False,
    )
```

```python
import functools
import math

import jax
import jax.numpy as jnp
from jax import lax
from jax.experimental import pallas as pl
from jax.experimental.pallas import tpu as pltpu
from jax.sharding import PartitionSpec as P

LEAF = 128
LEAVES = 2
F = 8
Q = 128
PAIRS_LEAF = 5
ML1 = 4
ML2 = 2
GROUP = 8
P_DEV = 256
PAIRS_MAX = 10

SOFT = 0.1
RADIUS_BOX = 1.0 + 0.5 * LEAVES
RADIUS_GROUP = 2.0 * RADIUS_BOX
ROWS = 2 * F
REC = 24
SPLIT = 3 * ROWS
BLOCK = 32
TOGETHER = 2
ROUNDER = 12582912.0

COS = (
    1.4142040807221545,
    -6.977642062283951,
    5.715238417642026,
    -1.728348665863032,
)
SIN = (
    4.442867902973949,
    -7.30744341898344,
    3.5947880563486,
    -0.7843739717150924,
)
MESH = pl.DeviceIdType.MESH


def horner(coefficients, z):
    total = coefficients[-1]
    for coefficient in coefficients[-2::-1]:
        total = total * z + coefficient
    return total


def geometry(target, cols):
    squared = SOFT * SOFT
    for axis in range(3):
        offset = target[axis] - cols[:, axis : axis + 1]
        squared = squared + offset * offset
    inverse = lax.rsqrt(squared)
    distance = squared * inverse
    distance = distance + (0.5 * inverse) * (squared - distance * distance)
    return distance, inverse


def point_terms(distance, inverse, turns, real, imag):
    phase = distance * turns
    phase = phase - ((phase + ROUNDER) - ROUNDER)
    z = phase * phase
    half_sine = phase * horner(SIN, z)
    scaled = inverse * half_sine
    cosine = inverse - scaled * half_sine
    sine = scaled * horner(COS, z)
    return cosine * real - sine * imag, cosine * imag + sine * real


def fold(block):
    return block.reshape(block.shape[0] // 8, 8, block.shape[1]).sum(0)


def apply_points(geo, spread, target, record, turns, add):
    values, xyz = record
    blocks = range(LEAF // BLOCK)
    for block in blocks:
        distance, inverse = geometry(target, xyz(block))
        geo[0, pl.ds(block * BLOCK, BLOCK), :] = distance
        geo[1, pl.ds(block * BLOCK, BLOCK), :] = inverse

    def frequencies(step, carry):
        for offset in range(TOGETHER):
            f = step * TOGETHER + offset
            wide = jnp.dot(values(), spread[f], preferred_element_type=jnp.float32)
            total_re, total_im = 0.0, 0.0
            for block in blocks:
                part = wide[block * BLOCK : (block + 1) * BLOCK]
                re, im = point_terms(
                    geo[0, pl.ds(block * BLOCK, BLOCK), :],
                    geo[1, pl.ds(block * BLOCK, BLOCK), :],
                    turns(f),
                    part[:, :128],
                    part[:, 128:],
                )
                total_re = total_re + fold(re)
                total_im = total_im + fold(im)
            add(f, total_re)
            add(F + f, total_im)
        return carry

    lax.fori_loop(0, F // TOGETHER, frequencies, 0)


def record_columns(rows):
    values = rows[:ROWS]
    high = values.astype(jnp.bfloat16).astype(jnp.float32)
    rest = values - high
    middle = rest.astype(jnp.bfloat16).astype(jnp.float32)
    low = rest - middle
    cols = jnp.concatenate([high, middle, low, rows[ROWS:]], axis=0).T
    return cols[:, :SPLIT].astype(jnp.bfloat16), cols[:, SPLIT:]


def adder(ref, first=False):
    def add(row, term):
        ref[row] = term if first else ref[row] + term

    return add


def rows_of(acc):
    return jnp.sum(acc, axis=1)


def wrapped(index, size):
    return jnp.where(index >= size, index - size, index)


def kernel(
    sec_size,
    dev_size,
    groups,
    wave_hbm,
    centers_hbm,
    group_centers_hbm,
    pairs_hbm,
    counts_hbm,
    lists_hbm,
    group_lists_hbm,
    sources_hbm,
    positions_hbm,
    weights_hbm,
    directions_hbm,
    fields_ref,
    rayleigh_ref,
    wave_ref,
    centers_ref,
    group_centers_ref,
    pairs_ref,
    counts_ref,
    lists_ref,
    group_lists_ref,
    sources_ref,
    positions_ref,
    weights_ref,
    directions_ref,
    geo,
    spread,
    acc,
    window,
    records,
    records_xyz,
    targets_xyz,
    scratch_rec,
    scratch_xyz,
    gathered,
    contribution,
    contributions,
    group_send,
    group_multipoles,
    local_send,
    group_locals,
    near,
    sums_send,
    sums,
    totals_send,
    totals,
    operand_sem,
    halo_send_sem,
    halo_recv_sem,
    wide_send_sem,
    wide_recv_sem,
    gather_send_sem,
    gather_recv_sem,
    up_send_sem,
    up_recv_sem,
    across_send_sem,
    across_recv_sem,
    down_send_sem,
    down_recv_sem,
    sums_send_sem,
    sums_recv_sem,
    totals_send_sem,
    totals_recv_sem,
):
    count = sec_size * dev_size
    sec, dev = lax.axis_index("sec"), lax.axis_index("dev")
    me = sec * dev_size + dev
    per_row = dev_size // GROUP
    group = me // GROUP
    member = dev % GROUP
    first = dev - member
    mates = [wrapped(member + step, GROUP) for step in range(1, GROUP)]
    mate_places = [(sec, first + mate) for mate in mates]
    far_places = [
        (wrapped(sec + row, sec_size), wrapped(dev + column * GROUP, dev_size))
        for row in range(sec_size)
        for column in range(per_row)
        if row or column
    ]
    last, begin = dev == dev_size - 1, dev == 0
    after = (
        jnp.where(last, wrapped(sec + 1, sec_size), sec),
        jnp.where(last, 0, dev + 1),
    )
    before = (
        jnp.where(begin, wrapped(sec + sec_size - 1, sec_size), sec),
        jnp.where(begin, dev_size - 1, dev - 1),
    )

    operands = [
        pltpu.make_async_copy(src, dst, operand_sem.at[index])
        for index, (src, dst) in enumerate(
            (
                (sources_hbm, sources_ref),
                (weights_hbm, weights_ref),
                (positions_hbm, positions_ref),
                (directions_hbm, directions_ref),
                (wave_hbm, wave_ref),
                (centers_hbm, centers_ref),
                (group_centers_hbm, group_centers_ref),
                (pairs_hbm, pairs_ref),
                (counts_hbm, counts_ref),
                (lists_hbm, lists_ref),
                (group_lists_hbm, group_lists_ref),
            )
        )
    ]
    for operand in operands:
        operand.start()

    barrier = pltpu.get_barrier_semaphore()
    partners = mate_places + far_places + [after, before]
    for partner in partners:
        pl.semaphore_signal(barrier, inc=1, device_id=partner, device_id_type=MESH)
    row = lax.broadcasted_iota(jnp.int32, (SPLIT, 256), 0) % ROWS
    column = lax.broadcasted_iota(jnp.int32, (SPLIT, 256), 1) // 128
    for f in range(F):
        spread[f] = jnp.where(row == f + F * column, 1.0, 0.0).astype(jnp.bfloat16)

    for operand in operands:
        operand.wait()

    def turns(f):
        return wave_ref[f] * (0.5 / math.pi)

    weighted = sources_ref[...] * weights_ref[...]
    own_rows = jnp.concatenate(
        [weighted, positions_ref[...], jnp.zeros((REC - ROWS - 3, P_DEV), jnp.float32)], axis=0
    )
    window[1] = own_rows
    for leaf in range(LEAVES):
        part = own_rows[:, leaf * LEAF : (leaf + 1) * LEAF]
        records[LEAVES + leaf], records_xyz[LEAVES + leaf] = record_columns(part)
        targets_xyz[leaf] = part[ROWS : ROWS + 8]
    directions = directions_ref[...]

    def proxies(centers, index, radius):
        return [centers[axis, index] + radius * directions[axis : axis + 1] for axis in range(3)]

    own_proxies = proxies(centers_ref, me, RADIUS_BOX)
    parent_proxies = proxies(group_centers_ref, group, RADIUS_GROUP)
    row_padding = jnp.zeros((REC - ROWS - 3, Q), jnp.float32)

    def set_records(slot, rows, xyz):
        scratch_rec[slot], scratch_xyz[slot] = record_columns(
            jnp.concatenate([rows, *xyz, row_padding], axis=0)
        )

    def loader(ref, index):
        xyz = records_xyz if ref is records else scratch_xyz
        return (
            lambda: ref[index],
            lambda block: xyz[index, pl.ds(block * BLOCK, BLOCK), :],
        )

    acc[...] = jnp.zeros_like(acc)

    def outward_leaf(leaf, carry):
        apply_points(geo, spread, own_proxies, loader(records, LEAVES + leaf), turns, adder(acc))
        return carry

    lax.fori_loop(0, LEAVES, outward_leaf, 0)
    own_multipole = rows_of(acc[...]) * (RADIUS_BOX / math.sqrt(P_DEV))
    gathered[member, group] = own_multipole

    pl.semaphore_wait(barrier, len(partners))

    halos = [
        pltpu.make_async_remote_copy(
            src_ref=window.at[1],
            dst_ref=window.at[slot],
            send_sem=halo_send_sem.at[way],
            recv_sem=halo_recv_sem.at[way],
            device_id=device,
            device_id_type=MESH,
        )
        for way, (slot, device) in enumerate(((0, after), (2, before)))
    ]
    for halo in halos:
        halo.start()

    def send_to(src, dst, send_sem, recv_sem, device):
        pltpu.make_async_remote_copy(
            src_ref=src,
            dst_ref=dst,
            send_sem=send_sem,
            recv_sem=recv_sem,
            device_id=device,
            device_id_type=MESH,
        ).start()

    def wait_bytes(ref, pieces, sem):
        part = ref.at[pl.ds(0, pieces)]
        pltpu.make_async_copy(part, part, sem).wait()

    own_slot = gathered.at[member, group]
    for device in far_places:
        send_to(own_slot, own_slot, wide_send_sem, wide_recv_sem, device)

    set_records(0, own_multipole, own_proxies)
    apply_points(geo, spread, parent_proxies, loader(scratch_rec, 0), turns, adder(acc, True))
    terms = rows_of(acc[...]) * (RADIUS_GROUP / math.sqrt(GROUP * Q))
    padding = jnp.zeros((6, Q), jnp.float32)
    for f in range(F):
        contribution[f] = jnp.concatenate(
            [terms[f : f + 1], terms[F + f : F + f + 1], padding], axis=0
        )
    contributions[member] = contribution[member]
    for mate, device in zip(mates, mate_places):
        send_to(
            contribution.at[mate], contributions.at[member], up_send_sem, up_recv_sem, device
        )

    for way, halo in enumerate(halos):
        halo.wait_recv()
        slot = 2 * way
        inside = jnp.where(me > 0, 1.0, 0.0) if way == 0 else jnp.where(me < count - 1, 1.0, 0.0)
        rows = window[slot]
        rows = jnp.concatenate([rows[:ROWS] * inside, rows[ROWS:]], axis=0)
        for leaf in range(LEAVES):
            index = slot * LEAVES + leaf
            records[index], records_xyz[index] = record_columns(
                rows[:, leaf * LEAF : (leaf + 1) * LEAF]
            )
    near[...] = jnp.zeros_like(near)

    def near_pair(pair, carry):
        target = pairs_ref[0, 0, pair]
        anchor = pairs_ref[0, 1, pair]
        live = jnp.where(pair < counts_ref[0], 1.0, 0.0)
        xyz = targets_xyz[target]
        lives = [jnp.where(target == leaf, live, 0.0) for leaf in range(LEAVES)]

        def add(row, term):
            for leaf in range(LEAVES):
                near[leaf, row] += term * lives[leaf]

        apply_points(
            geo, spread, [xyz[axis : axis + 1] for axis in range(3)], loader(records, anchor), turns, add
        )
        return carry

    first_half = PAIRS_MAX // 2
    lax.fori_loop(0, first_half, near_pair, 0)

    wait_bytes(contributions, GROUP - 1, up_recv_sem)
    total = contributions[0]
    for other in range(1, GROUP):
        total = total + contributions[other]
    group_send[...] = total
    group_multipoles[group] = total

    for device in far_places:
        send_to(
            group_send, group_multipoles.at[group], across_send_sem, across_recv_sem, device
        )

    if groups > 1:
        wait_bytes(gathered.at[0], groups - 1, wide_recv_sem)
    own_part = gathered.at[member]
    for device in mate_places:
        send_to(own_part, own_part, gather_send_sem, gather_recv_sem, device)

    lax.fori_loop(first_half, PAIRS_MAX, near_pair, 0)

    if groups > 1:
        wait_bytes(group_multipoles, groups - 1, across_recv_sem)
    my_turns = turns(member)
    local_re, local_im = 0.0, 0.0
    for m in range(ML2):
        other = group_lists_ref[m, group]
        rows = group_multipoles[other]
        xyz = proxies(group_centers_ref, other, RADIUS_GROUP)
        cols = jnp.concatenate([rows, *xyz, row_padding], axis=0).T
        for block in range(Q // BLOCK):
            part = cols[block * BLOCK : (block + 1) * BLOCK]
            distance, inverse = geometry(parent_proxies, part[:, 8:16])
            re, im = point_terms(distance, inverse, my_turns, part[:, 0:1], part[:, 1:2])
            local_re = local_re + fold(re)
            local_im = local_im + fold(im)
    local_rows = [jnp.sum(part, axis=0, keepdims=True) for part in (local_re, local_im)]
    local = jnp.concatenate([*local_rows, padding], axis=0) * (
        RADIUS_GROUP / math.sqrt(ML2 * Q)
    )
    local_send[...] = local
    group_locals[member] = local

    for device in mate_places:
        send_to(local_send, group_locals.at[member], down_send_sem, down_recv_sem, device)

    wait_bytes(gathered, GROUP - 1, gather_recv_sem)
    acc[...] = jnp.zeros_like(acc)

    def list_box(m, carry):
        other = lists_ref[0, m]
        set_records(
            0, gathered[other % GROUP, other // GROUP], proxies(centers_ref, other, RADIUS_BOX)
        )
        apply_points(geo, spread, own_proxies, loader(scratch_rec, 0), turns, adder(acc))
        return carry

    lax.fori_loop(0, ML1, list_box, 0)
    incoming = rows_of(acc[...]) * (RADIUS_BOX / math.sqrt(ML1 * Q))

    wait_bytes(group_locals, GROUP - 1, down_recv_sem)
    rows = jnp.concatenate(
        [group_locals[f][part : part + 1] for part in range(2) for f in range(F)], axis=0
    )
    set_records(0, rows, parent_proxies)
    apply_points(geo, spread, own_proxies, loader(scratch_rec, 0), turns, adder(acc, True))
    descended = rows_of(acc[...]) * (RADIUS_GROUP / math.sqrt(Q))
    set_records(0, incoming + descended, own_proxies)

    def far_leaf(leaf, carry):
        xyz = targets_xyz[leaf]

        def add(row, term):
            near[leaf, row] = near[leaf, row] * (1.0 / math.sqrt(LEAF * PAIRS_LEAF)) + term * (
                RADIUS_BOX / math.sqrt(Q)
            )

        apply_points(
            geo, spread, [xyz[axis : axis + 1] for axis in range(3)], loader(scratch_rec, 0), turns, add
        )
        return carry

    lax.fori_loop(0, LEAVES, far_leaf, 0)
    sources = sources_ref[...]
    fields = jnp.concatenate([rows_of(near[leaf]) for leaf in range(LEAVES)], axis=1)
    fields_ref[...] = fields
    result = 0.5 * sources + fields

    s_re, s_im = sources[:F], sources[F:]
    r_re, r_im = result[:F], result[F:]
    real_sum = jnp.sum(s_re * r_re + s_im * r_im, axis=1, keepdims=True)
    imag_sum = jnp.sum(s_re * r_im - s_im * r_re, axis=1, keepdims=True)
    squares = jnp.sum(s_re * s_re + s_im * s_im, axis=1, keepdims=True)
    lane = lax.broadcasted_iota(jnp.int32, (F, 128), 1)
    mine = jnp.where(
        lane == 0, real_sum, jnp.where(lane == 1, imag_sum, jnp.where(lane == 2, squares, 0.0))
    )
    sums_send[...] = mine
    sums[member] = mine
    for device in mate_places:
        send_to(sums_send, sums.at[member], sums_send_sem, sums_recv_sem, device)

    for halo in halos:
        halo.wait_send()
    if groups > 1:
        wait_bytes(gathered.at[0], groups - 1, wide_send_sem)
        wait_bytes(group_multipoles, groups - 1, across_send_sem)
    wait_bytes(gathered, GROUP - 1, gather_send_sem)
    wait_bytes(contributions, GROUP - 1, up_send_sem)
    wait_bytes(group_locals, GROUP - 1, down_send_sem)

    wait_bytes(sums, GROUP - 1, sums_recv_sem)
    total = jnp.sum(sums[...], axis=0)
    totals_send[...] = total
    totals[group] = total
    for device in far_places:
        send_to(totals_send, totals.at[group], totals_send_sem, totals_recv_sem, device)
    wait_bytes(sums, GROUP - 1, sums_send_sem)
    if groups > 1:
        wait_bytes(totals, groups - 1, totals_recv_sem)
    total = jnp.sum(totals[...], axis=0).T
    rayleigh_ref[...] = total[0:2, :] / (total[2:3, :] + 1e-06)
    if groups > 1:
        wait_bytes(totals, groups - 1, totals_send_sem)


def on_device(
    sec_size,
    dev_size,
    sources,
    positions,
    weights,
    wavenumbers,
    directions,
    box_centers,
    group_centers,
    near_pairs,
    pair_counts,
    box_lists,
    group_lists,
):
    count = sec_size * dev_size
    groups = count // GROUP
    hbm = pl.BlockSpec(memory_space=pltpu.HBM)
    vmem = pl.BlockSpec(memory_space=pltpu.VMEM)
    f32 = jnp.float32
    fields, rayleigh = pl.pallas_call(
        functools.partial(kernel, sec_size, dev_size, groups),
        out_shape=(
            jax.ShapeDtypeStruct((ROWS, P_DEV), f32),
            jax.ShapeDtypeStruct((2, F), f32),
        ),
        in_specs=[hbm] * 11,
        out_specs=(vmem, vmem),
        scratch_shapes=[
            pltpu.SMEM((F,), f32),
            pltpu.SMEM((3, count), f32),
            pltpu.SMEM((3, groups), f32),
            pltpu.SMEM((1, 2, PAIRS_MAX), jnp.int32),
            pltpu.SMEM((1,), jnp.int32),
            pltpu.SMEM((1, ML1), jnp.int32),
            pltpu.SMEM((ML2, groups), jnp.int32),
            pltpu.VMEM((ROWS, P_DEV), f32),
            pltpu.VMEM((3, P_DEV), f32),
            pltpu.VMEM((1, P_DEV), f32),
            pltpu.VMEM((3, Q), f32),
            pltpu.VMEM((2, LEAF, 128), f32),
            pltpu.VMEM((F, SPLIT, 256), jnp.bfloat16),
            pltpu.VMEM((ROWS, 8, 128), f32),
            pltpu.VMEM((3, REC, P_DEV), f32),
            pltpu.VMEM((3 * LEAVES, LEAF, SPLIT), jnp.bfloat16),
            pltpu.VMEM((3 * LEAVES, LEAF, REC - ROWS), f32),
            pltpu.VMEM((LEAVES, 8, LEAF), f32),
            pltpu.VMEM((1, Q, SPLIT), jnp.bfloat16),
            pltpu.VMEM((1, Q, REC - ROWS), f32),
            pltpu.VMEM((GROUP, groups, ROWS, Q), f32),
            pltpu.VMEM((F, 8, Q), f32),
            pltpu.VMEM((GROUP, 8, Q), f32),
            pltpu.VMEM((8, Q), f32),
            pltpu.VMEM((groups, 8, Q), f32),
            pltpu.VMEM((8, Q), f32),
            pltpu.VMEM((GROUP, 8, Q), f32),
            pltpu.VMEM((LEAVES, ROWS, 8, LEAF), f32),
            pltpu.VMEM((F, 128), f32),
            pltpu.VMEM((GROUP, F, 128), f32),
            pltpu.VMEM((F, 128), f32),
            pltpu.VMEM((groups, F, 128), f32),
            pltpu.SemaphoreType.DMA((11,)),
            pltpu.SemaphoreType.DMA((2,)),
            pltpu.SemaphoreType.DMA((2,)),
        ]
        + [pltpu.SemaphoreType.DMA] * 14,
        compiler_params=pltpu.CompilerParams(
            collective_id=0, has_side_effects=True, vmem_limit_bytes=63 * 1024 * 1024
        ),
        name="bem_matvec",
    )(
        wavenumbers,
        box_centers,
        group_centers,
        near_pairs,
        pair_counts,
        box_lists,
        group_lists.T,
        sources.reshape(ROWS, P_DEV),
        positions,
        weights[None, :],
        directions,
    )
    return 0.5 * sources + fields.reshape(2, F, P_DEV), rayleigh


def solution(mesh):
    in_specs = (
        P(None, None, ("sec", "dev")),
        P(None, ("sec", "dev")),
        P(("sec", "dev")),
        P(),
        P(),
        P(),
        P(),
        P(("sec", "dev"), None, None),
        P(("sec", "dev")),
        P(("sec", "dev"), None),
        P(),
    )
    out_specs = (P(None, None, ("sec", "dev")), P())
    return jax.shard_map(
        functools.partial(on_device, mesh.shape["sec"], mesh.shape["dev"]),
        mesh=mesh,
        in_specs=in_specs,
        out_specs=out_specs,
        check_vma=False,
    )
```

```python
import functools
import math

import jax
import jax.numpy as jnp
from jax import lax
from jax.experimental import pallas as pl
from jax.experimental.pallas import tpu as pltpu
from jax.sharding import PartitionSpec as P

LEAF = 128
LEAVES = 2
F = 8
Q = 128
PAIRS_LEAF = 5
ML1 = 4
ML2 = 2
GROUP = 8
P_DEV = 256
PAIRS_MAX = 10

SOFT = 0.1
RADIUS_BOX = 1.0 + 0.5 * LEAVES
RADIUS_GROUP = 2.0 * RADIUS_BOX
ROWS = 2 * F
REC = 24
SPLIT = 3 * ROWS
BLOCK = 32
JOBS = 2
ROUNDER = 12582912.0

COS = (
    1.4142040807221545,
    -6.977642062283951,
    5.715238417642026,
    -1.728348665863032,
)
SIN = (
    4.442867902973949,
    -7.30744341898344,
    3.5947880563486,
    -0.7843739717150924,
)
MESH = pl.DeviceIdType.MESH


def horner(coefficients, z):
    total = coefficients[-1]
    for coefficient in coefficients[-2::-1]:
        total = total * z + coefficient
    return total


def geometry(target, cols):
    squared = SOFT * SOFT
    for axis in range(3):
        offset = target[axis] - cols[:, axis : axis + 1]
        squared = squared + offset * offset
    inverse = lax.rsqrt(squared)
    distance = squared * inverse
    distance = distance + (0.5 * inverse) * (squared - distance * distance)
    return distance, inverse


def point_terms(distance, inverse, turns, real, imag):
    phase = distance * turns
    phase = phase - ((phase + ROUNDER) - ROUNDER)
    z = phase * phase
    half_sine = phase * horner(SIN, z)
    scaled = inverse * half_sine
    cosine = inverse - scaled * half_sine
    sine = scaled * horner(COS, z)
    return cosine * real - sine * imag, cosine * imag + sine * real


def fold(block):
    return block.reshape(block.shape[0] // 8, 8, block.shape[1]).sum(0)


def apply_points(geo, spread, turns, jobs):
    blocks = [pl.ds(start, BLOCK) for start in range(0, LEAF, BLOCK)]
    for slot, (target, (_, xyz), _) in enumerate(jobs):
        for block in blocks:
            distance, inverse = geometry(target, xyz(block))
            geo[2 * slot, block, :] = distance
            geo[2 * slot + 1, block, :] = inverse
    for f in range(F):
        for slot, (_, (values, _), add) in enumerate(jobs):
            wide = jnp.dot(values(), spread[f], preferred_element_type=jnp.float32)
            total_re, total_im = 0.0, 0.0
            for block in blocks:
                part = wide[block.start : block.start + BLOCK]
                re, im = point_terms(
                    geo[2 * slot, block, :],
                    geo[2 * slot + 1, block, :],
                    turns[f],
                    part[:, :128],
                    part[:, 128:],
                )
                total_re = total_re + fold(re)
                total_im = total_im + fold(im)
            add(f, total_re)
            add(F + f, total_im)


def record_columns(rows):
    values = rows[:ROWS]
    high = values.astype(jnp.bfloat16).astype(jnp.float32)
    rest = values - high
    middle = rest.astype(jnp.bfloat16).astype(jnp.float32)
    low = rest - middle
    cols = jnp.concatenate([high, middle, low, rows[ROWS:]], axis=0).T
    return cols[:, :SPLIT].astype(jnp.bfloat16), cols[:, SPLIT:]


def adder(ref, first=False):
    def add(row, term):
        ref[row] = term if first else ref[row] + term

    return add


def rows_of(acc):
    return jnp.sum(acc, axis=1)


def wrapped(index, size):
    return jnp.where(index >= size, index - size, index)


def kernel(
    sec_size,
    dev_size,
    groups,
    wave_hbm,
    centers_hbm,
    group_centers_hbm,
    pairs_hbm,
    counts_hbm,
    lists_hbm,
    group_lists_hbm,
    sources_hbm,
    positions_hbm,
    weights_hbm,
    directions_hbm,
    fields_ref,
    rayleigh_ref,
    wave_ref,
    centers_ref,
    group_centers_ref,
    pairs_ref,
    counts_ref,
    lists_ref,
    group_lists_ref,
    sources_ref,
    positions_ref,
    weights_ref,
    directions_ref,
    geo,
    spread,
    acc,
    window,
    records,
    records_xyz,
    targets_xyz,
    scratch_rec,
    scratch_xyz,
    gathered,
    contribution,
    contributions,
    group_send,
    group_multipoles,
    local_send,
    group_locals,
    near,
    sums_send,
    sums,
    totals_send,
    totals,
    operand_sem,
    halo_send_sem,
    halo_recv_sem,
    wide_send_sem,
    wide_recv_sem,
    gather_send_sem,
    gather_recv_sem,
    up_send_sem,
    up_recv_sem,
    across_send_sem,
    across_recv_sem,
    down_send_sem,
    down_recv_sem,
    sums_send_sem,
    sums_recv_sem,
    totals_send_sem,
    totals_recv_sem,
):
    count = sec_size * dev_size
    sec, dev = lax.axis_index("sec"), lax.axis_index("dev")
    me = sec * dev_size + dev
    per_row = dev_size // GROUP
    group = me // GROUP
    member = dev % GROUP
    first = dev - member
    mates = [wrapped(member + step, GROUP) for step in range(1, GROUP)]
    mate_places = [(sec, first + mate) for mate in mates]
    far_places = [
        (wrapped(sec + row, sec_size), wrapped(dev + column * GROUP, dev_size))
        for row in range(sec_size)
        for column in range(per_row)
        if row or column
    ]
    last, begin = dev == dev_size - 1, dev == 0
    after = (
        jnp.where(last, wrapped(sec + 1, sec_size), sec),
        jnp.where(last, 0, dev + 1),
    )
    before = (
        jnp.where(begin, wrapped(sec + sec_size - 1, sec_size), sec),
        jnp.where(begin, dev_size - 1, dev - 1),
    )

    operands = [
        pltpu.make_async_copy(src, dst, operand_sem.at[index])
        for index, (src, dst) in enumerate(
            (
                (sources_hbm, sources_ref),
                (weights_hbm, weights_ref),
                (positions_hbm, positions_ref),
                (directions_hbm, directions_ref),
                (wave_hbm, wave_ref),
                (centers_hbm, centers_ref),
                (group_centers_hbm, group_centers_ref),
                (pairs_hbm, pairs_ref),
                (counts_hbm, counts_ref),
                (lists_hbm, lists_ref),
                (group_lists_hbm, group_lists_ref),
            )
        )
    ]
    for operand in operands:
        operand.start()

    barrier = pltpu.get_barrier_semaphore()
    partners = mate_places + far_places + [after, before]
    for partner in partners:
        pl.semaphore_signal(barrier, inc=1, device_id=partner, device_id_type=MESH)
    row = lax.broadcasted_iota(jnp.int32, (SPLIT, 256), 0) % ROWS
    column = lax.broadcasted_iota(jnp.int32, (SPLIT, 256), 1) // 128
    for f in range(F):
        spread[f] = jnp.where(row == f + F * column, 1.0, 0.0).astype(jnp.bfloat16)

    for operand in operands:
        operand.wait()

    turns = [wave_ref[f] * (0.5 / math.pi) for f in range(F)]

    weighted = sources_ref[...] * weights_ref[...]
    own_rows = jnp.concatenate(
        [weighted, positions_ref[...], jnp.zeros((REC - ROWS - 3, P_DEV), jnp.float32)], axis=0
    )
    window[1] = own_rows
    for leaf in range(LEAVES):
        part = own_rows[:, leaf * LEAF : (leaf + 1) * LEAF]
        records[LEAVES + leaf], records_xyz[LEAVES + leaf] = record_columns(part)
        targets_xyz[leaf] = part[ROWS : ROWS + 8]
    directions = directions_ref[...]

    def proxies(centers, index, radius):
        return [centers[axis, index] + radius * directions[axis : axis + 1] for axis in range(3)]

    own_proxies = proxies(centers_ref, me, RADIUS_BOX)
    parent_proxies = proxies(group_centers_ref, group, RADIUS_GROUP)
    row_padding = jnp.zeros((REC - ROWS - 3, Q), jnp.float32)

    def set_records(slot, rows, xyz):
        scratch_rec[slot], scratch_xyz[slot] = record_columns(
            jnp.concatenate([rows, *xyz, row_padding], axis=0)
        )

    def loader(ref, index):
        xyz = records_xyz if ref is records else scratch_xyz
        return (
            lambda: ref[index],
            lambda block: xyz[index, block, :],
        )

    acc[...] = jnp.zeros_like(acc)
    apply_points(
        geo,
        spread,
        turns,
        [
            (own_proxies, loader(records, LEAVES + leaf), adder(acc))
            for leaf in range(LEAVES)
        ],
    )
    own_multipole = rows_of(acc[...]) * (RADIUS_BOX / math.sqrt(P_DEV))
    gathered[member, group] = own_multipole

    pl.semaphore_wait(barrier, len(partners))

    halos = [
        pltpu.make_async_remote_copy(
            src_ref=window.at[1],
            dst_ref=window.at[slot],
            send_sem=halo_send_sem.at[way],
            recv_sem=halo_recv_sem.at[way],
            device_id=device,
            device_id_type=MESH,
        )
        for way, (slot, device) in enumerate(((0, after), (2, before)))
    ]
    for halo in halos:
        halo.start()

    def send_to(src, dst, send_sem, recv_sem, device):
        pltpu.make_async_remote_copy(
            src_ref=src,
            dst_ref=dst,
            send_sem=send_sem,
            recv_sem=recv_sem,
            device_id=device,
            device_id_type=MESH,
        ).start()

    def wait_bytes(ref, pieces, sem):
        part = ref.at[pl.ds(0, pieces)]
        pltpu.make_async_copy(part, part, sem).wait()

    own_slot = gathered.at[member, group]
    for device in far_places:
        send_to(own_slot, own_slot, wide_send_sem, wide_recv_sem, device)

    set_records(0, own_multipole, own_proxies)
    apply_points(
        geo, spread, turns, [(parent_proxies, loader(scratch_rec, 0), adder(acc, True))]
    )
    terms = rows_of(acc[...]) * (RADIUS_GROUP / math.sqrt(GROUP * Q))
    padding = jnp.zeros((6, Q), jnp.float32)
    for f in range(F):
        contribution[f] = jnp.concatenate(
            [terms[f : f + 1], terms[F + f : F + f + 1], padding], axis=0
        )
    contributions[member] = contribution[member]
    for mate, device in zip(mates, mate_places):
        send_to(
            contribution.at[mate], contributions.at[member], up_send_sem, up_recv_sem, device
        )

    for way, halo in enumerate(halos):
        halo.wait_recv()
        slot = 2 * way
        inside = jnp.where(me > 0, 1.0, 0.0) if way == 0 else jnp.where(me < count - 1, 1.0, 0.0)
        rows = window[slot]
        rows = jnp.concatenate([rows[:ROWS] * inside, rows[ROWS:]], axis=0)
        for leaf in range(LEAVES):
            index = slot * LEAVES + leaf
            records[index], records_xyz[index] = record_columns(
                rows[:, leaf * LEAF : (leaf + 1) * LEAF]
            )
    near[...] = jnp.zeros_like(near)

    def near_job(pair):
        target = pairs_ref[0, 0, pair]
        anchor = pairs_ref[0, 1, pair]
        live = jnp.where(pair < counts_ref[0], 1.0, 0.0)
        xyz = targets_xyz[target]
        lives = [jnp.where(target == leaf, live, 0.0) for leaf in range(LEAVES)]

        def add(row, term):
            for leaf in range(LEAVES):
                near[leaf, row] += term * lives[leaf]

        return [xyz[axis : axis + 1] for axis in range(3)], loader(records, anchor), add

    def near_turn(turn, carry):
        apply_points(
            geo, spread, turns, [near_job(turn * JOBS + offset) for offset in range(JOBS)]
        )
        return carry

    near_turns = PAIRS_MAX // JOBS
    first_half = (near_turns + 1) // 2
    lax.fori_loop(0, first_half, near_turn, 0)

    wait_bytes(contributions, GROUP - 1, up_recv_sem)
    total = contributions[0]
    for other in range(1, GROUP):
        total = total + contributions[other]
    group_send[...] = total
    group_multipoles[group] = total

    for device in far_places:
        send_to(
            group_send, group_multipoles.at[group], across_send_sem, across_recv_sem, device
        )

    if groups > 1:
        wait_bytes(gathered.at[0], groups - 1, wide_recv_sem)
    own_part = gathered.at[member]
    for device in mate_places:
        send_to(own_part, own_part, gather_send_sem, gather_recv_sem, device)

    lax.fori_loop(first_half, near_turns, near_turn, 0)

    if groups > 1:
        wait_bytes(group_multipoles, groups - 1, across_recv_sem)
    my_turns = wave_ref[member] * (0.5 / math.pi)
    local_re, local_im = 0.0, 0.0
    for m in range(ML2):
        other = group_lists_ref[m, group]
        rows = group_multipoles[other]
        xyz = proxies(group_centers_ref, other, RADIUS_GROUP)
        cols = jnp.concatenate([rows, *xyz, row_padding], axis=0).T
        for block in range(Q // BLOCK):
            part = cols[block * BLOCK : (block + 1) * BLOCK]
            distance, inverse = geometry(parent_proxies, part[:, 8:16])
            re, im = point_terms(distance, inverse, my_turns, part[:, 0:1], part[:, 1:2])
            local_re = local_re + fold(re)
            local_im = local_im + fold(im)
    local_rows = [jnp.sum(part, axis=0, keepdims=True) for part in (local_re, local_im)]
    local = jnp.concatenate([*local_rows, padding], axis=0) * (
        RADIUS_GROUP / math.sqrt(ML2 * Q)
    )
    local_send[...] = local
    group_locals[member] = local

    for device in mate_places:
        send_to(local_send, group_locals.at[member], down_send_sem, down_recv_sem, device)

    wait_bytes(gathered, GROUP - 1, gather_recv_sem)
    acc[...] = jnp.zeros_like(acc)

    def list_boxes(turn, carry):
        jobs = []
        for slot in range(JOBS):
            other = lists_ref[0, turn * JOBS + slot]
            set_records(
                slot,
                gathered[other % GROUP, other // GROUP],
                proxies(centers_ref, other, RADIUS_BOX),
            )
            jobs.append((own_proxies, loader(scratch_rec, slot), adder(acc)))
        apply_points(geo, spread, turns, jobs)
        return carry

    lax.fori_loop(0, ML1 // JOBS, list_boxes, 0)
    incoming = rows_of(acc[...]) * (RADIUS_BOX / math.sqrt(ML1 * Q))

    wait_bytes(group_locals, GROUP - 1, down_recv_sem)
    rows = jnp.concatenate(
        [group_locals[f][part : part + 1] for part in range(2) for f in range(F)], axis=0
    )
    set_records(0, rows, parent_proxies)
    apply_points(geo, spread, turns, [(own_proxies, loader(scratch_rec, 0), adder(acc, True))])
    descended = rows_of(acc[...]) * (RADIUS_GROUP / math.sqrt(Q))
    set_records(0, incoming + descended, own_proxies)

    def far_job(leaf):
        xyz = targets_xyz[leaf]

        def add(row, term):
            near[leaf, row] = near[leaf, row] * (1.0 / math.sqrt(LEAF * PAIRS_LEAF)) + term * (
                RADIUS_BOX / math.sqrt(Q)
            )

        return [xyz[axis : axis + 1] for axis in range(3)], loader(scratch_rec, 0), add

    apply_points(geo, spread, turns, [far_job(leaf) for leaf in range(LEAVES)])
    sources = sources_ref[...]
    fields = jnp.concatenate([rows_of(near[leaf]) for leaf in range(LEAVES)], axis=1)
    fields_ref[...] = fields
    result = 0.5 * sources + fields

    s_re, s_im = sources[:F], sources[F:]
    r_re, r_im = result[:F], result[F:]
    real_sum = jnp.sum(s_re * r_re + s_im * r_im, axis=1, keepdims=True)
    imag_sum = jnp.sum(s_re * r_im - s_im * r_re, axis=1, keepdims=True)
    squares = jnp.sum(s_re * s_re + s_im * s_im, axis=1, keepdims=True)
    lane = lax.broadcasted_iota(jnp.int32, (F, 128), 1)
    mine = jnp.where(
        lane == 0, real_sum, jnp.where(lane == 1, imag_sum, jnp.where(lane == 2, squares, 0.0))
    )
    sums_send[...] = mine
    sums[member] = mine
    for device in mate_places:
        send_to(sums_send, sums.at[member], sums_send_sem, sums_recv_sem, device)

    for halo in halos:
        halo.wait_send()
    if groups > 1:
        wait_bytes(gathered.at[0], groups - 1, wide_send_sem)
        wait_bytes(group_multipoles, groups - 1, across_send_sem)
    wait_bytes(gathered, GROUP - 1, gather_send_sem)
    wait_bytes(contributions, GROUP - 1, up_send_sem)
    wait_bytes(group_locals, GROUP - 1, down_send_sem)

    wait_bytes(sums, GROUP - 1, sums_recv_sem)
    total = jnp.sum(sums[...], axis=0)
    totals_send[...] = total
    totals[group] = total
    for device in far_places:
        send_to(totals_send, totals.at[group], totals_send_sem, totals_recv_sem, device)
    wait_bytes(sums, GROUP - 1, sums_send_sem)
    if groups > 1:
        wait_bytes(totals, groups - 1, totals_recv_sem)
    total = jnp.sum(totals[...], axis=0).T
    rayleigh_ref[...] = total[0:2, :] / (total[2:3, :] + 1e-06)
    if groups > 1:
        wait_bytes(totals, groups - 1, totals_send_sem)


def on_device(
    sec_size,
    dev_size,
    sources,
    positions,
    weights,
    wavenumbers,
    directions,
    box_centers,
    group_centers,
    near_pairs,
    pair_counts,
    box_lists,
    group_lists,
):
    count = sec_size * dev_size
    groups = count // GROUP
    hbm = pl.BlockSpec(memory_space=pltpu.HBM)
    vmem = pl.BlockSpec(memory_space=pltpu.VMEM)
    f32 = jnp.float32
    fields, rayleigh = pl.pallas_call(
        functools.partial(kernel, sec_size, dev_size, groups),
        out_shape=(
            jax.ShapeDtypeStruct((ROWS, P_DEV), f32),
            jax.ShapeDtypeStruct((2, F), f32),
        ),
        in_specs=[hbm] * 11,
        out_specs=(vmem, vmem),
        scratch_shapes=[
            pltpu.SMEM((F,), f32),
            pltpu.SMEM((3, count), f32),
            pltpu.SMEM((3, groups), f32),
            pltpu.SMEM((1, 2, PAIRS_MAX), jnp.int32),
            pltpu.SMEM((1,), jnp.int32),
            pltpu.SMEM((1, ML1), jnp.int32),
            pltpu.SMEM((ML2, groups), jnp.int32),
            pltpu.VMEM((ROWS, P_DEV), f32),
            pltpu.VMEM((3, P_DEV), f32),
            pltpu.VMEM((1, P_DEV), f32),
            pltpu.VMEM((3, Q), f32),
            pltpu.VMEM((2 * JOBS, LEAF, 128), f32),
            pltpu.VMEM((F, SPLIT, 256), jnp.bfloat16),
            pltpu.VMEM((ROWS, 8, 128), f32),
            pltpu.VMEM((3, REC, P_DEV), f32),
            pltpu.VMEM((3 * LEAVES, LEAF, SPLIT), jnp.bfloat16),
            pltpu.VMEM((3 * LEAVES, LEAF, REC - ROWS), f32),
            pltpu.VMEM((LEAVES, 8, LEAF), f32),
            pltpu.VMEM((JOBS, Q, SPLIT), jnp.bfloat16),
            pltpu.VMEM((JOBS, Q, REC - ROWS), f32),
            pltpu.VMEM((GROUP, groups, ROWS, Q), f32),
            pltpu.VMEM((F, 8, Q), f32),
            pltpu.VMEM((GROUP, 8, Q), f32),
            pltpu.VMEM((8, Q), f32),
            pltpu.VMEM((groups, 8, Q), f32),
            pltpu.VMEM((8, Q), f32),
            pltpu.VMEM((GROUP, 8, Q), f32),
            pltpu.VMEM((LEAVES, ROWS, 8, LEAF), f32),
            pltpu.VMEM((F, 128), f32),
            pltpu.VMEM((GROUP, F, 128), f32),
            pltpu.VMEM((F, 128), f32),
            pltpu.VMEM((groups, F, 128), f32),
            pltpu.SemaphoreType.DMA((11,)),
            pltpu.SemaphoreType.DMA((2,)),
            pltpu.SemaphoreType.DMA((2,)),
        ]
        + [pltpu.SemaphoreType.DMA] * 14,
        compiler_params=pltpu.CompilerParams(
            collective_id=0, has_side_effects=True, vmem_limit_bytes=63 * 1024 * 1024
        ),
        name="bem_matvec",
    )(
        wavenumbers,
        box_centers,
        group_centers,
        near_pairs,
        pair_counts,
        box_lists,
        group_lists.T,
        sources.reshape(ROWS, P_DEV),
        positions,
        weights[None, :],
        directions,
    )
    return 0.5 * sources + fields.reshape(2, F, P_DEV), rayleigh


def solution(mesh):
    in_specs = (
        P(None, None, ("sec", "dev")),
        P(None, ("sec", "dev")),
        P(("sec", "dev")),
        P(),
        P(),
        P(),
        P(),
        P(("sec", "dev"), None, None),
        P(("sec", "dev")),
        P(("sec", "dev"), None),
        P(),
    )
    out_specs = (P(None, None, ("sec", "dev")), P())
    return jax.shard_map(
        functools.partial(on_device, mesh.shape["sec"], mesh.shape["dev"]),
        mesh=mesh,
        in_specs=in_specs,
        out_specs=out_specs,
        check_vma=False,
    )
```
